128 devices in a mesh: dp: 32 (over z, y, core), head: 4 (over x).
Axes of the slice: x: 4, y: 4, z: 4, core: 2. Of those that a mesh axis runs over, the one named last changes fastest.
Arguments:
- hidden: bfloat16 [16384, 4096], P('dp', 'head'), may hold values from -10 to 10
- query_weight: bfloat16 [4096, 2048], P('head'), as said below
- key_weight: bfloat16 [4096, 2048], P(None, 'head'), as said below
- value_weight: bfloat16 [4096, 2048], P(None, 'head'), may hold values from -0.09375 to 0.09375
- output_weight: bfloat16 [2048, 4096], P(None, 'head'), may hold values from -0.125 to 0.125
- encoded: bfloat16 [128, 128, 4096], P('dp'), may hold values from -10 to 10
- location: int32 [128], replicated, may hold values from 0 to 127, as said below
- neighbours: int32 [256, 2], P('dp'), may hold values from 0 to 127, as said below
- pattern: int32 [256, 2], P('dp'), may hold values from 0 to 1, as said below
- grad_out: bfloat16 [16384, 4096], P('dp', 'head'), may hold values from -6 to 6
Outputs:
- attended: bfloat16 [16384, 4096], P('dp', 'head')
- grad_hidden: bfloat16 [16384, 4096], P('dp', 'head')
- grad_encoded: bfloat16 [128, 128, 4096], P(('dp', 'head'))
The draws below stay inside these ranges and needn't reach their ends.
Inputs may be any that keep to these rules, and one draw needn't show every extreme that they name: A permutation: the encoded tokens of database row r are encoded[location[r]]. `neighbours`: database row ids. Group the storage indices into aligned blocks of 4 (same s // 4); for every sequence, at most 2 of its 16 entries name rows stored in one block, and they name at most 1 distinct rows; in every draw each sequence names some row twice. `pattern`: every span attends at least one neighbour. `query_weight`: entries of order 4096 ** -0.5. `key_weight`: entries of order 4096 ** -0.5.
All inputs are finite; a program needn't handle non-finite values.
Results may differ from the reference program's by a relative error of at most 0.04.
Values may be sent and summed in bfloat16 or wider, within the bound.
A program may use at most 192 MiB of HBM per device.

```python
import math
import jax
import jax.numpy as jnp
from jax import lax

D = 4096
HD = 128
SPAN = 64
NTOK = 128
NBR = 2
HEADS = 16
SPANS_DEV = 8
ROWS_DEV = 4
SEQ = 512
SPANS = 256
TOKENS = 16384
ROWS = 128
HW = 2048
N_DP = 32
N_HEAD = 4


def index_tables(key):
    locations = jax.random.permutation(jax.random.fold_in(key, 101), ROWS).astype(jnp.int32)
    inverse = jnp.argsort(locations).astype(jnp.int32)
    owner_count = ROWS // ROWS_DEV
    slot_count = SPANS_DEV * NBR
    hot_source = (jax.random.randint(jax.random.fold_in(key, 102), (owner_count,), 0, 4) == 0).astype(jnp.int32)
    owner_keys = jax.random.split(jax.random.fold_in(key, 103), owner_count)
    pair_low = max(1, slot_count - owner_count)
    pair_high = min(slot_count // 2, pair_low + 3)

    def one_owner(owner_key):
        key_pairs, key_order, key_score, key_within, key_second, key_forced, key_extra = jax.random.split(owner_key, 7)
        pair_count = jax.random.randint(key_pairs, (), pair_low, pair_high + 1)
        slot_index = jnp.arange(slot_count)
        group_of = jnp.where(slot_index < 2 * pair_count, slot_index // 2, slot_index - pair_count)
        order_perm = jax.random.permutation(key_order, slot_count)
        slot_group = group_of[order_perm]
        source_score = jax.random.randint(key_score, (owner_count,), 0, 4096) + hot_source * 4096
        ranked = jnp.argsort(-(source_score * owner_count + jnp.arange(owner_count)))
        within = jnp.minimum(jax.random.randint(key_within, (slot_count,), 0, ROWS_DEV), jax.random.randint(key_second, (slot_count,), 0, ROWS_DEV))
        group_source = ranked[jnp.minimum(slot_index, owner_count - 1)]
        group_stored = group_source * ROWS_DEV + within
        row_ids = inverse[group_stored[slot_group]]
        forced_live = jax.random.randint(key_forced, (SPANS_DEV,), 0, NBR)
        extra_live = jax.random.randint(key_extra, (SPANS_DEV, NBR), 0, 4) > 0
        live_flags = (jnp.arange(NBR)[None, :] == forced_live[:, None]) | extra_live
        return (row_ids.reshape(SPANS_DEV, NBR), live_flags.astype(jnp.int32), forced_live)
    row_ids, live_flags, forced_live = jax.vmap(one_owner)(owner_keys)
    return (locations, row_ids.reshape(SPANS, NBR).astype(jnp.int32), live_flags.reshape(SPANS, NBR), forced_live.reshape(SPANS).astype(jnp.int32))


def draw_location(key, part):
    tables = index_tables(key)
    return tables[0]


def draw_neighbours(key, part):
    tables = index_tables(key)
    return tables[1]


def draw_pattern(key, part):
    tables = index_tables(key)
    return tables[2]


def draw_encoded(key, part):
    key = jax.random.fold_in(key, 4)
    return jnp.clip(jax.random.normal(key, (ROWS, NTOK, D), jnp.float32), -6.0, 6.0).astype(jnp.bfloat16)


def draw_hidden(key, part):
    key = jax.random.fold_in(key, 6)
    return jnp.clip(jax.random.normal(key, (TOKENS, D), jnp.float32), -6.0, 6.0).astype(jnp.bfloat16)


def draw_query_weight(key, part):
    key = jax.random.fold_in(key, 9)
    return (jnp.clip(jax.random.normal(key, (D, HW), jnp.float32), -6.0, 6.0) / math.sqrt(D)).astype(jnp.bfloat16)


def draw_key_weight(key, part):
    key = jax.random.fold_in(key, 10)
    own_draw = jnp.clip(jax.random.normal(key, (D, HW), jnp.float32), -6.0, 6.0) / math.sqrt(D)
    return own_draw.astype(jnp.bfloat16)


def shard_levels(rng, dims, cuts, least, top_value):
    gain, own = 1.0, jax.random.fold_in(rng, 6)
    for dim, shards_of in cuts:
        steps = jnp.exp(jax.random.uniform(jax.random.fold_in(own, dim), (shards_of,), jnp.float32, least / len(cuts), top_value / len(cuts)))
        gain = gain * jnp.repeat(steps, dims[dim] // shards_of).reshape([-1 if axis == dim else 1 for axis in range(len(dims))])
    return gain


def gaussian(key, dims, width, bound, pieces=(), held_as=jnp.bfloat16):
    loudness = shard_levels(key, dims, pieces, -0.22, 0.18) if pieces else 1.0
    entries = jax.random.normal(key, dims, jnp.float32) * width * loudness
    return jnp.minimum(jnp.maximum(entries, -bound), bound).astype(held_as)


def setup_inputs(seed: int = 0) -> dict:
    keys = jax.random.split(jax.random.key(seed), 11)
    hidden = draw_hidden(jax.random.fold_in(keys[10], 71), 0)
    query_weight = draw_query_weight(jax.random.fold_in(keys[10], 71), 0)
    key_weight = draw_key_weight(jax.random.fold_in(keys[10], 71), 0)
    value_weight = gaussian(keys[3], (D, HW), D ** -0.5, 0.09375, ((1, 4),))
    output_weight = gaussian(keys[4], (HW, D), HW ** -0.5, 0.125, ((1, 4),))
    encoded = draw_encoded(jax.random.fold_in(keys[10], 71), 0)
    location = draw_location(jax.random.fold_in(keys[10], 71), 0)
    neighbours = draw_neighbours(jax.random.fold_in(keys[10], 71), 0)
    pattern = draw_pattern(jax.random.fold_in(keys[10], 71), 0)
    grad_out = gaussian(keys[9], (TOKENS, D), 1.0, 6.0, ((0, 32), (1, 4)))
    return {"hidden": hidden, "query_weight": query_weight, "key_weight": key_weight, "value_weight": value_weight, "output_weight": output_weight, "encoded": encoded, "location": location, "neighbours": neighbours, "pattern": pattern, "grad_out": grad_out}


def shift_up(tensor_in):
    padding = jnp.zeros((SPAN - 1,) + tensor_in.shape[1:], tensor_in.dtype)
    return jnp.concatenate([tensor_in[SPAN - 1:], padding], axis=0)


def shift_down(tensor_in):
    padding = jnp.zeros((SPAN - 1,) + tensor_in.shape[1:], tensor_in.dtype)
    return jnp.concatenate([padding, tensor_in[: tensor_in.shape[0] - SPAN + 1]], axis=0)


def gather_memory(table, stored):
    picked = jnp.take(table, stored, axis=0)
    return picked.reshape(SPANS_DEV, NBR * NTOK, HEADS, HD)


def forward_probs(query_block, key_block, live_flags, score_scale):
    scores = jnp.einsum("cqhd,cmhd->chqm", query_block.astype(jnp.float32), key_block.astype(jnp.float32)) * score_scale
    live_mask = jnp.repeat(live_flags, NTOK, axis=1)[:, None, None, :] > 0
    masked = jnp.where(live_mask, scores, -1e30)
    row_max = jnp.max(masked, axis=-1, keepdims=True)
    exp_terms = jnp.where(live_mask, jnp.exp(masked - row_max), 0.0)
    return exp_terms / jnp.sum(exp_terms, axis=-1, keepdims=True)


def reference(hidden, query_weight, key_weight, value_weight, output_weight, encoded, location, neighbours, pattern, grad_out):
    score_scale = HD ** -0.5
    queries = jnp.dot(hidden, query_weight, preferred_element_type=jnp.float32).astype(jnp.bfloat16)
    state_rows = encoded.reshape(ROWS * NTOK, D)
    key_rows = jnp.dot(state_rows, key_weight, preferred_element_type=jnp.float32).astype(jnp.bfloat16).reshape(ROWS, NTOK, HW)
    value_rows = jnp.dot(state_rows, value_weight, preferred_element_type=jnp.float32).astype(jnp.bfloat16).reshape(ROWS, NTOK, HW)
    grad_blended = jnp.dot(grad_out, output_weight.T, preferred_element_type=jnp.float32).astype(jnp.bfloat16)

    def one_sequence(accumulated, sequence):
        tok_start = sequence * SEQ
        span_start = sequence * SPANS_DEV
        seq_queries = lax.dynamic_slice_in_dim(queries, tok_start, SEQ, 0)
        seq_grads = lax.dynamic_slice_in_dim(grad_blended, tok_start, SEQ, 0)
        row_ids = lax.dynamic_slice_in_dim(neighbours, span_start, SPANS_DEV, 0)
        live_flags = lax.dynamic_slice_in_dim(pattern, span_start, SPANS_DEV, 0)
        stored = jnp.take(location, row_ids.reshape(-1), axis=0).astype(jnp.int32)
        key_block = gather_memory(key_rows, stored)
        value_block = gather_memory(value_rows, stored)
        query_block = shift_up(seq_queries).reshape(SPANS_DEV, SPAN, HEADS, HD)
        grad_block = shift_up(seq_grads).reshape(SPANS_DEV, SPAN, HEADS, HD)
        soft_weights = forward_probs(query_block, key_block, live_flags, score_scale)
        rounded = soft_weights.astype(jnp.bfloat16)
        blended = jnp.einsum("chqm,cmhd->cqhd", rounded.astype(jnp.float32), value_block.astype(jnp.float32)).astype(jnp.bfloat16)
        blended = shift_down(blended.reshape(SEQ, HW))
        grad_weights = jnp.einsum("cqhd,cmhd->chqm", grad_block.astype(jnp.float32), value_block.astype(jnp.float32))
        inner_sum = jnp.sum(soft_weights * grad_weights, axis=-1, keepdims=True)
        grad_scores = (soft_weights * (grad_weights - inner_sum) * score_scale).astype(jnp.bfloat16)
        grad_queries = jnp.einsum("chqm,cmhd->cqhd", grad_scores.astype(jnp.float32), key_block.astype(jnp.float32)).astype(jnp.bfloat16)
        grad_queries = shift_down(grad_queries.reshape(SEQ, HW))
        key_slot = jnp.einsum("chqm,cqhd->cmhd", grad_scores.astype(jnp.float32), query_block.astype(jnp.float32))
        value_slot = jnp.einsum("chqm,cqhd->cmhd", rounded.astype(jnp.float32), grad_block.astype(jnp.float32))
        slot_grads = jnp.concatenate([key_slot.reshape(SPANS_DEV * NBR, NTOK * HW), value_slot.reshape(SPANS_DEV * NBR, NTOK * HW)], axis=1)
        one_hot = (jnp.arange(ROWS, dtype=jnp.int32)[:, None] == stored[None, :]).astype(jnp.float32)
        row_term = jnp.dot(one_hot, slot_grads, precision=lax.Precision.HIGHEST, preferred_element_type=jnp.float32)
        row_term = lax.optimization_barrier(row_term.astype(jnp.bfloat16)).astype(jnp.float32)
        return accumulated + row_term, (blended, grad_queries)

    start_acc = jnp.zeros((ROWS, 2 * NTOK * HW), jnp.float32)
    accumulated, outputs = lax.scan(one_sequence, start_acc, jnp.arange(N_DP, dtype=jnp.int32))
    blended_all = outputs[0].reshape(TOKENS, HW)
    grad_queries_all = outputs[1].reshape(TOKENS, HW)
    row_grads = accumulated.astype(jnp.bfloat16)
    key_grad = row_grads[:, : NTOK * HW].reshape(ROWS * NTOK, HW)
    value_grad = row_grads[:, NTOK * HW:].reshape(ROWS * NTOK, HW)
    group_width = HW // N_HEAD
    running = jnp.zeros((ROWS * NTOK, D), jnp.float32)
    for group_index in range(N_HEAD):
        lower = group_index * group_width
        upper = lower + group_width
        group_term = jnp.dot(key_grad[:, lower:upper], key_weight[:, lower:upper].T, preferred_element_type=jnp.float32)
        group_term = group_term + jnp.dot(value_grad[:, lower:upper], value_weight[:, lower:upper].T, preferred_element_type=jnp.float32)
        running = running + lax.optimization_barrier(group_term.astype(jnp.bfloat16)).astype(jnp.float32)
    grad_encoded = running.astype(jnp.bfloat16).reshape(ROWS, NTOK, D)
    attended = jnp.dot(blended_all, output_weight, preferred_element_type=jnp.float32).astype(jnp.bfloat16)
    grad_hidden = jnp.dot(grad_queries_all, query_weight.T, preferred_element_type=jnp.float32).astype(jnp.bfloat16)
    return attended, grad_hidden, grad_encoded
```

```python
import functools

import jax
import jax.numpy as jnp
from jax import lax
from jax.experimental import pallas as pl
from jax.experimental.pallas import tpu as pltpu
from jax.sharding import PartitionSpec as P

HD = 128
SPAN = 64
NTOK = 128
MESH = pl.DeviceIdType.MESH
BF = jnp.bfloat16
F32 = jnp.float32
NEG = -1e30
SCALE = HD**-0.5
ANY = pl.BlockSpec(memory_space=pl.ANY)
VM = pl.BlockSpec(memory_space=pltpu.VMEM)
SM = pl.BlockSpec(memory_space=pltpu.SMEM)
CHUNKS = 4
TC = NTOK // CHUNKS


def dot(a, b, ca, cb):
    return lax.dot_general(a, b, (((ca,), (cb,)), ((), ())), preferred_element_type=F32)


class Ring:
    def __init__(self, me, place):
        self.me = me
        self.p = me + 1 - 2 * (me % 2)
        self.q = 3 - me
        self.far = (me + 2) % 4
        self.dev_p = place(self.p)
        self.dev_q = place(self.q)
        self.dev_far = place(self.far)


def rings():
    dp = lax.axis_index("dp")
    x = lax.axis_index("head")
    z, y, c = dp // 8, (dp // 2) % 4, dp % 2
    ring_z = Ring(z, lambda v: ((v * 4 + y) * 2 + c, x))
    ring_y = Ring(y, lambda v: ((z * 4 + v) * 2 + c, x))
    ring_x = Ring(x, lambda v: (dp, v))
    sister = ((z * 4 + y) * 2 + 1 - c, x)
    return ring_z, ring_y, ring_x, sister, c


def greet(devices):
    barrier = pltpu.get_barrier_semaphore()
    for device in devices:
        pl.semaphore_signal(barrier, inc=1, device_id=device, device_id_type=MESH)
    pl.semaphore_wait(barrier, len(devices))


class Copies:
    def __init__(self, send, recv, local):
        self.send, self.recv, self.local = send, recv, local
        self.remote_count = self.local_count = 0
        self.started = []

    def push(self, src, dst, device):
        index = self.remote_count
        self.remote_count += 1
        copy = pltpu.make_async_remote_copy(
            src_ref=src,
            dst_ref=dst,
            send_sem=self.send.at[index],
            recv_sem=self.recv.at[index],
            device_id=device,
            device_id_type=MESH,
        )
        copy.start()
        self.started.append(copy)
        return copy

    def move(self, src, dst):
        index = self.local_count
        self.local_count += 1
        copy = pltpu.make_async_copy(src, dst, self.local.at[index])
        copy.start()
        return copy

    def finish(self):
        for copy in self.started:
            copy.wait_send()


class Reduce:
    def __init__(self, copies, ring, part, tmp, got):
        self.copies, self.ring, self.part, self.tmp, self.got = copies, ring, part, tmp, got

    def start(self):
        r, part = self.ring, self.part
        self.to_far = (
            self.copies.push(part(r.far, 0), self.tmp(0), r.dev_p),
            self.copies.push(part(r.far, 1), self.tmp(1), r.dev_q),
        )
        self.near = (
            self.copies.push(part(r.p, 0), self.got(0), r.dev_p),
            self.copies.push(part(r.q, 1), self.got(3), r.dev_q),
        )

    def relay(self, add):
        r, part = self.ring, self.part
        self.to_far[0].wait_recv()
        add(part(r.q, 0), part(r.q, 0), self.tmp(0))
        first = self.copies.push(part(r.q, 0), self.got(2), r.dev_q)
        self.to_far[1].wait_recv()
        add(part(r.p, 1), part(r.p, 1), self.tmp(1))
        second = self.copies.push(part(r.p, 1), self.got(1), r.dev_p)
        self.near = self.near + (first, second)

    def end(self, add, own):
        for copy in self.near:
            copy.wait_recv()
        add(own(0), self.part(self.ring.me, 0), self.got(0), self.got(2))
        add(own(1), self.part(self.ring.me, 1), self.got(1), self.got(3))


class Gather:
    def __init__(self, copies, ring, slot):
        self.copies, self.ring, self.slot = copies, ring, slot

    def start(self, own):
        r = self.ring
        self.to_p = self.copies.push(own, self.slot(r.me), r.dev_p)
        self.to_q = self.copies.push(own, self.slot(r.me), r.dev_q)

    def relay_p(self):
        r = self.ring
        self.to_p.wait_recv()
        self.fwd_q = self.copies.push(self.slot(r.p, 0), self.slot(r.p, 0), r.dev_q)

    def relay_q(self):
        r = self.ring
        self.to_q.wait_recv()
        self.fwd_p = self.copies.push(self.slot(r.q, 1), self.slot(r.q, 1), r.dev_p)

    def relay(self):
        self.relay_p()
        self.relay_q()

    def end(self):
        self.fwd_q.wait_recv()
        self.fwd_p.wait_recv()


def add_rows(out, *terms):
    lead = out.shape[0]
    if len(out.shape) == 3:
        for index in range(lead):
            total = terms[0][index].astype(F32)
            for term in terms[1:]:
                total = total + term[index].astype(F32)
            out[index] = total.astype(out.dtype)
        return
    step = 32

    def block(i, carry):
        rows = pl.ds(pl.multiple_of(i * step, step), step)
        total = terms[0][rows].astype(F32)
        for term in terms[1:]:
            total = total + term[rows].astype(F32)
        out[rows] = total.astype(out.dtype)
        return carry

    lax.fori_loop(0, lead // step, block, 0)


def fetch_kernel(
    hid, wq, enc, wk, wv, gout, wo, ids,
    qg_out, rows_out, ids_out,
    v_hid, v_wq, v_enc, v_wk, v_wv, v_gout, v_wo, part, tmp, got, own, kv, send, recv, local,
):
    ring_z, ring_y, ring_x, sister, c = rings()
    copies = Copies(send, recv, local)
    loads = [
        copies.move(a, b)
        for a, b in (
            (hid, v_hid), (wq, v_wq), (enc, v_enc), (wk, v_wk), (wv, v_wv), (gout, v_gout), (wo, v_wo),
        )
    ]
    greet(
        [ring_x.dev_p, ring_x.dev_q, ring_y.dev_p, ring_y.dev_q, ring_z.dev_p, ring_z.dev_q, ring_z.dev_far, sister]
    )
    id_copies = [
        copies.push(ids, ids_out.at[ring_z.me], d) for d in (ring_z.dev_p, ring_z.dev_q, ring_z.dev_far)
    ]
    locals_left = [copies.move(ids, ids_out.at[ring_z.me])]

    def rows_of(unit, half):
        return pl.ds((unit % 2) * 256 + half * 128, 128)

    def unit_of(u):
        w = u // 2
        reduce = Reduce(
            copies,
            ring_x,
            lambda i, half: part.at[w, i, rows_of(u, half)],
            lambda half: tmp.at[u, half],
            lambda k: got.at[u, k],
        )

        def slot(i, half=None):
            rows = pl.ds((u % 2) * 256, 256) if half is None else rows_of(u, half)
            return qg_out.at[w, i, rows]

        return reduce, Gather(copies, ring_z, slot)

    units = [unit_of(u) for u in range(4)]

    def own_part(u):
        return lambda half: own.at[u // 2, rows_of(u, half)]

    def reduced(u):
        reduce, gather = units[u]
        reduce.end(add_rows, own_part(u))
        block = own.at[u // 2, pl.ds((u % 2) * 256, 256)]
        gather.start(block)
        locals_left.append(copies.move(block, gather.slot(ring_z.me)))

    loads[0].wait()
    loads[1].wait()

    def query_tile(g, carry):
        cols = pl.ds(pl.multiple_of(g * 512, 512), 512)
        part[0, g] = dot(v_hid[...], v_wq[:, cols], 1, 0).astype(BF)
        return carry

    lax.fori_loop(0, 4, query_tile, 0)
    units[0][0].start()
    units[1][0].start()

    streams = []
    loads[2].wait()
    for s, weight in ((0, v_wk), (1, v_wv)):
        loads[3 + s].wait()

        def row_tile(i, carry):
            rows = pl.ds(pl.multiple_of(i * 256, 256), 256)
            kv[s, rows] = dot(v_enc[rows, :], weight[...], 1, 0).astype(BF)
            return carry

        lax.fori_loop(0, 2, row_tile, 0)

        def slot(i, half=None, s=s):
            block = rows_out.at[i * 2 + c, s]
            return block if half is None else block.at[pl.ds((half + s) % 2 * 256, 256)]

        gather = Gather(copies, ring_y, slot)
        gather.start(kv.at[s])
        to_sister = [copies.push(kv.at[s], slot(ring_y.me), sister)]
        locals_left.append(copies.move(kv.at[s], slot(ring_y.me)))
        streams.append((gather, to_sister))

    units[0][0].relay(add_rows)
    loads[5].wait()
    loads[6].wait()

    def grad_tile(g, carry):
        rows = pl.ds(pl.multiple_of(g * 512, 512), 512)
        part[1, g] = dot(v_gout[...], v_wo[rows, :], 1, 1).astype(BF)
        return carry

    lax.fori_loop(0, 4, grad_tile, 0)
    units[2][0].start()
    reduced(0)
    units[1][0].relay(add_rows)
    units[3][0].start()
    reduced(1)
    units[0][1].relay()
    units[2][0].relay(add_rows)

    def forward(s):
        gather, to_sister = streams[s]
        gather.relay_p()
        to_sister.append(copies.push(gather.slot(ring_y.p), gather.slot(ring_y.p), sister))
        gather.relay_q()
        to_sister.append(copies.push(gather.slot(ring_y.q), gather.slot(ring_y.q), sister))

    forward(0)
    reduced(2)
    units[1][1].relay()
    units[3][0].relay(add_rows)
    forward(1)
    reduced(3)
    units[2][1].relay()
    for gather, to_sister in streams:
        gather.fwd_q.wait_recv()
        to_sister.append(copies.push(gather.slot(ring_y.far, 0), gather.slot(ring_y.far, 0), sister))
        gather.fwd_p.wait_recv()
        to_sister.append(copies.push(gather.slot(ring_y.far, 1), gather.slot(ring_y.far, 1), sister))
    units[3][1].relay()
    for _, gather in units:
        gather.end()
    for _, to_sister in streams:
        for copy in to_sister:
            copy.wait_recv()
    for copy in id_copies:
        copy.wait_recv()
    for copy in locals_left:
        copy.wait()
    copies.finish()


def fetch(hid, wq, enc, wk, wv, gout, wo, ids):
    return pl.pallas_call(
        fetch_kernel,
        out_shape=[
            jax.ShapeDtypeStruct((2, 4, 512, 512), BF),
            jax.ShapeDtypeStruct((8, 2, 512, 512), BF),
            jax.ShapeDtypeStruct((4, 8, 128), jnp.int32),
        ],
        in_specs=[ANY] * 8,
        out_specs=[ANY] * 3,
        scratch_shapes=[
            pltpu.VMEM((512, 1024), BF),
            pltpu.VMEM((1024, 2048), BF),
            pltpu.VMEM((512, 4096), BF),
            pltpu.VMEM((4096, 512), BF),
            pltpu.VMEM((4096, 512), BF),
            pltpu.VMEM((512, 1024), BF),
            pltpu.VMEM((2048, 1024), BF),
            pltpu.VMEM((2, 4, 512, 512), BF),
            pltpu.VMEM((4, 2, 128, 512), BF),
            pltpu.VMEM((4, 4, 128, 512), BF),
            pltpu.VMEM((2, 512, 512), BF),
            pltpu.VMEM((2, 512, 512), BF),
            pltpu.SemaphoreType.DMA((64,)),
            pltpu.SemaphoreType.DMA((64,)),
            pltpu.SemaphoreType.DMA((16,)),
        ],
        compiler_params=pltpu.CompilerParams(
            collective_id=0, has_side_effects=True, vmem_limit_bytes=52 << 20
        ),
        name="project_and_gather",
    )(hid, wq, enc, wk, wv, gout, wo, ids)


def slot_of(ids_ref, loc_ref, index, k):
    entry = ids_ref[index // 8, index % 8, k]
    stored = loc_ref[entry % 256]
    z = lax.axis_index("dp") // 8
    live = jnp.logical_and(entry >= 256, stored // 32 == z)
    return live, stored % 32


def two_heads(block):
    zero = jnp.zeros((SPAN, HD), BF)
    return jnp.concatenate(
        [
            jnp.concatenate([block[:, :HD], zero], axis=1),
            jnp.concatenate([zero, block[:, HD:]], axis=1),
        ],
        axis=0,
    )


def stats_kernel(ids_ref, loc_ref, qg_ref, rows_ref, stats_ref):
    stats_ref[0] = jnp.full((64, 128), NEG, F32)
    stats_ref[1] = jnp.zeros((64, 128), F32)
    stats_ref[2] = jnp.zeros((64, 128), F32)

    def span(i, carry):
        for k in range(2):
            live, row = slot_of(ids_ref, loc_ref, i, k)

            @pl.when(live)
            def _():
                for pair in range(2):
                    cols = pl.ds(pair * 256, 256)
                    key = rows_ref[row // 4, 0, row % 4, :, cols]
                    value = rows_ref[row // 4, 1, row % 4, :, cols]
                    s = dot(key, two_heads(qg_ref[0, i, :, cols]), 1, 1) * SCALE
                    gw = dot(value, two_heads(qg_ref[1, i, :, cols]), 1, 1)
                    line = pl.ds(i * 2 + pair, 1)
                    top = jnp.max(s, axis=0, keepdims=True)
                    old = stats_ref[0, line, :]
                    new = jnp.maximum(top, old)
                    e = jnp.exp(s - new)
                    fade = jnp.exp(old - new)
                    stats_ref[0, line, :] = new
                    stats_ref[1, line, :] = stats_ref[1, line, :] * fade + jnp.sum(e, axis=0, keepdims=True)
                    stats_ref[2, line, :] = stats_ref[2, line, :] * fade + jnp.sum(e * gw, axis=0, keepdims=True)

        return carry

    lax.fori_loop(0, 32, span, 0)


def stats_of(ids, loc, qg, rows):
    return pl.pallas_call(
        stats_kernel,
        out_shape=jax.ShapeDtypeStruct((3, 64, 128), F32),
        in_specs=[SM, SM, VM, VM],
        out_specs=VM,
        compiler_params=pltpu.CompilerParams(vmem_limit_bytes=52 << 20),
        name="span_stats",
    )(ids, loc, qg, rows)


def combine_kernel(stats_ref, out_ref, held, send, recv):
    ring_z, _, _, _, _ = rings()
    others = (ring_z.dev_p, ring_z.dev_q, ring_z.dev_far)
    greet(others)
    copies = Copies(send, recv, None)
    pushed = [copies.push(stats_ref, held.at[k], device) for k, device in enumerate(others)]
    for copy in pushed:
        copy.wait_recv()
    tops = [stats_ref[0]] + [held[k, 0] for k in range(3)]
    sums = [stats_ref[1]] + [held[k, 1] for k in range(3)]
    dots = [stats_ref[2]] + [held[k, 2] for k in range(3)]
    top = jnp.maximum(jnp.maximum(tops[0], tops[1]), jnp.maximum(tops[2], tops[3]))
    fades = [jnp.exp(t - top) for t in tops]
    total = sum(f * s for f, s in zip(fades, sums))
    inner = sum(f * d for f, d in zip(fades, dots))
    out_ref[0] = top
    out_ref[1] = 1.0 / total
    out_ref[2] = inner / total
    copies.finish()


def combine(stats):
    return pl.pallas_call(
        combine_kernel,
        out_shape=jax.ShapeDtypeStruct((3, 64, 128), F32),
        in_specs=[VM],
        out_specs=VM,
        scratch_shapes=[
            pltpu.VMEM((3, 3, 64, 128), F32),
            pltpu.SemaphoreType.DMA((3,)),
            pltpu.SemaphoreType.DMA((3,)),
        ],
        compiler_params=pltpu.CompilerParams(collective_id=1, has_side_effects=True),
        name="combine_stats",
    )(stats)


def attend_kernel(ids_ref, loc_ref, qg_ref, rows_ref, stats_ref, og_ref, grads_ref):
    def clear(i, carry):
        for s in range(2):
            for r in range(4):
                grads_ref[i, s, r] = jnp.zeros((NTOK, 512), BF)
        return carry

    lax.fori_loop(0, 8, clear, 0)

    def span(i, carry):
        og_ref[0, i] = jnp.zeros((SPAN, 512), BF)
        og_ref[1, i] = jnp.zeros((SPAN, 512), BF)
        for k in range(2):
            live, row = slot_of(ids_ref, loc_ref, i, k)

            @pl.when(live)
            def _():
                for pair in range(2):
                    cols = pl.ds(pair * 256, 256)
                    key = rows_ref[row // 4, 0, row % 4, :, cols]
                    value = rows_ref[row // 4, 1, row % 4, :, cols]
                    query = two_heads(qg_ref[0, i, :, cols])
                    grad = two_heads(qg_ref[1, i, :, cols])
                    line = pl.ds(i * 2 + pair, 1)
                    s = dot(key, query, 1, 1) * SCALE
                    gw = dot(value, grad, 1, 1)
                    w = jnp.exp(s - stats_ref[0, line, :]) * stats_ref[1, line, :]
                    ds = (w * (gw - stats_ref[2, line, :]) * SCALE).astype(BF)
                    w = w.astype(BF)
                    for which, probs, memory, other in ((0, w, value, grad), (1, ds, key, query)):
                        out = dot(probs, memory, 0, 0)
                        for h in range(2):
                            head = pl.ds(pair * 256 + h * HD, HD)
                            part = out[h * SPAN : (h + 1) * SPAN, h * HD : (h + 1) * HD]
                            og_ref[which, i, :, head] = (
                                og_ref[which, i, :, head].astype(F32) + part
                            ).astype(BF)
                        s_index = 1 - which
                        grads_ref[row // 4, s_index, row % 4, :, cols] = (
                            grads_ref[row // 4, s_index, row % 4, :, cols].astype(F32)
                            + dot(probs, other, 1, 0)
                        ).astype(BF)

        return carry

    lax.fori_loop(0, 32, span, 0)


def attend(ids, loc, qg, rows, stats):
    return pl.pallas_call(
        attend_kernel,
        out_shape=[
            jax.ShapeDtypeStruct((2, 32, SPAN, 512), BF),
            jax.ShapeDtypeStruct((8, 2, 4, NTOK, 512), BF),
        ],
        in_specs=[SM, SM, VM, VM, VM],
        out_specs=[VM, VM],
        compiler_params=pltpu.CompilerParams(vmem_limit_bytes=52 << 20),
        name="attend_both_ways",
    )(ids, loc, qg, rows, stats)


def return_kernel(
    og_part, grads, wk, wv, wo, wq,
    attended, grad_hidden, grad_encoded,
    v_wk, v_wv, v_wo, v_wq, og, z_tmp, z_got, own, everyone, rg, c_got, y_tmp, y_got, mine, term, x_tmp, x_got,
    send, recv, local,
):
    ring_z, ring_y, ring_x, sister, c = rings()
    copies = Copies(send, recv, local)
    og_loads = [copies.move(og_part.at[w], og.at[w]) for w in range(2)]
    order = (ring_y.far, ring_y.p, ring_y.q, ring_y.me)
    rg_loads = [
        [
            copies.move(grads.at[i * 2 + c, :, :, pl.ds(t * TC, TC)], rg.at[i, :, :, pl.ds(t * TC, TC)])
            for i in order
        ]
        for t in range(CHUNKS)
    ]
    weight_loads = [copies.move(a, b) for a, b in ((wk, v_wk), (wv, v_wv), (wo, v_wo), (wq, v_wq))]
    greet([ring_x.dev_p, ring_x.dev_q, ring_y.dev_p, ring_y.dev_q, ring_z.dev_p, ring_z.dev_q, sister])
    swaps = [
        [
            copies.push(
                grads.at[i * 2 + 1 - c, :, :, pl.ds(t * TC, TC)],
                c_got.at[i, :, :, pl.ds(t * TC, TC)],
                sister,
            )
            for i in order
        ]
        for t in range(CHUNKS)
    ]

    def rows_of(unit, half):
        return pl.ds((unit % 2) * 256 + half * 128, 128)

    def z_unit(u):
        w = u // 2
        reduce = Reduce(
            copies,
            ring_z,
            lambda i, half: og.at[w, i, rows_of(u, half)],
            lambda half: z_tmp.at[u, half],
            lambda k: z_got.at[u, k],
        )

        def slot(i, half=None):
            rows = pl.ds((u % 2) * 256, 256) if half is None else rows_of(u, half)
            return everyone.at[w, i, rows]

        return reduce, Gather(copies, ring_x, slot)

    def y_unit(t):
        rows = pl.ds(t * TC, TC)
        by_row = Reduce(
            copies,
            ring_y,
            lambda i, half: rg.at[i, half, :, rows],
            lambda half: y_tmp.at[half, :, rows],
            lambda k: y_got.at[k, :, rows],
        )
        by_group = Reduce(
            copies,
            ring_x,
            lambda i, half: term.at[i, rows, pl.ds(half * 2048, 2048)],
            lambda half: x_tmp.at[half, rows],
            lambda k: x_got.at[k, rows],
        )
        return by_row, by_group

    z_units = [z_unit(u) for u in range(4)]
    y_units = [y_unit(t) for t in range(CHUNKS)]

    def z_done(u):
        reduce, gather = z_units[u]
        reduce.end(add_rows, lambda half: own.at[u // 2, rows_of(u, half)])
        block = own.at[u // 2, pl.ds((u % 2) * 256, 256)]
        gather.start(block)
        everyone[u // 2, ring_x.me, pl.ds((u % 2) * 256, 256)] = block[...]

    def y_start(t):
        rows = pl.ds(t * TC, TC)
        for k, i in enumerate(order):
            rg_loads[t][k].wait()
            swaps[t][k].wait_recv()
            for half in range(2):
                block = rg.at[i, half, :, rows]
                add_rows(block, block, c_got.at[i, half, :, rows])
        y_units[t][0].start()

    def y_done(t):
        rows = pl.ds(t * TC, TC)
        y_units[t][0].end(add_rows, lambda half: mine.at[half, :, rows])
        if t == 0:
            weight_loads[0].wait()
            weight_loads[1].wait()

        def tile(j, carry):
            cols = pl.ds(pl.multiple_of(j * 512, 512), 512)
            keys = mine[0, :, rows, :].reshape(4 * TC, 512)
            values = mine[1, :, rows, :].reshape(4 * TC, 512)
            product = dot(keys, v_wk[cols, :], 1, 1) + dot(values, v_wv[cols, :], 1, 1)
            term[:, rows, cols] = product.astype(BF).reshape(4, TC, 512)
            return carry

        lax.fori_loop(0, 8, tile, 0)
        y_units[t][1].start()

    for w in range(2):
        og_loads[w].wait()
    z_units[0][0].start()
    y_start(0)
    z_units[1][0].start()
    y_start(1)
    for k in range(4):
        z_units[k][0].relay(add_rows)
        y_units[k][0].relay(add_rows)
        if k + 2 < 4:
            z_units[k + 2][0].start()
            y_start(k + 2)
        y_done(k)
        z_done(k)
        if k >= 1:
            y_units[k - 1][1].relay(add_rows)
            z_units[k - 1][1].relay()
    y_units[3][1].relay(add_rows)
    z_units[3][1].relay()

    weight_loads[2].wait()
    weight_loads[3].wait()

    def result(t):
        rows = pl.ds(t * TC, TC)
        y_units[t][1].end(add_rows, lambda half: grad_encoded.at[rows, pl.ds(half * 2048, 2048)])

    def attended_tile(i, carry):
        rows = pl.ds(pl.multiple_of(i * 128, 128), 128)
        total = dot(everyone[0, 0, rows, :], v_wo[0:512, :], 1, 0)
        for g in range(1, 4):
            total = total + dot(everyone[0, g, rows, :], v_wo[g * 512 : (g + 1) * 512, :], 1, 0)
        attended[rows, :] = total.astype(BF)
        return carry

    def hidden_tile(i, carry):
        rows = pl.ds(pl.multiple_of(i * 128, 128), 128)
        total = dot(everyone[1, 0, rows, :], v_wq[:, 0:512], 1, 1)
        for g in range(1, 4):
            total = total + dot(everyone[1, g, rows, :], v_wq[:, g * 512 : (g + 1) * 512], 1, 1)
        grad_hidden[rows, :] = total.astype(BF)
        return carry

    result(0)
    result(1)
    z_units[0][1].end()
    z_units[1][1].end()
    lax.fori_loop(0, 4, attended_tile, 0)
    result(2)
    result(3)
    z_units[2][1].end()
    z_units[3][1].end()
    lax.fori_loop(0, 4, hidden_tile, 0)
    copies.finish()


def give_back(og_part, grads, wk, wv, wo, wq):
    return pl.pallas_call(
        return_kernel,
        out_shape=[
            jax.ShapeDtypeStruct((512, 1024), BF),
            jax.ShapeDtypeStruct((512, 1024), BF),
            jax.ShapeDtypeStruct((NTOK, 4096), BF),
        ],
        in_specs=[ANY] * 6,
        out_specs=[VM] * 3,
        scratch_shapes=[
            pltpu.VMEM((4096, 512), BF),
            pltpu.VMEM((4096, 512), BF),
            pltpu.VMEM((2048, 1024), BF),
            pltpu.VMEM((1024, 2048), BF),
            pltpu.VMEM((2, 4, 512, 512), BF),
            pltpu.VMEM((4, 2, 128, 512), BF),
            pltpu.VMEM((4, 4, 128, 512), BF),
            pltpu.VMEM((2, 512, 512), BF),
            pltpu.VMEM((2, 4, 512, 512), BF),
            pltpu.VMEM((4, 2, 4, NTOK, 512), BF),
            pltpu.VMEM((4, 2, 4, NTOK, 512), BF),
            pltpu.VMEM((2, 4, NTOK, 512), BF),
            pltpu.VMEM((4, 4, NTOK, 512), BF),
            pltpu.VMEM((2, 4, NTOK, 512), BF),
            pltpu.VMEM((4, NTOK, 4096), BF),
            pltpu.VMEM((2, NTOK, 2048), BF),
            pltpu.VMEM((4, NTOK, 2048), BF),
            pltpu.SemaphoreType.DMA((112,)),
            pltpu.SemaphoreType.DMA((112,)),
            pltpu.SemaphoreType.DMA((32,)),
        ],
        compiler_params=pltpu.CompilerParams(
            collective_id=2, has_side_effects=True, vmem_limit_bytes=60 << 20
        ),
        name="reduce_and_project",
    )(og_part, grads, wk, wv, wo, wq)


def shift_up(rows):
    return jnp.pad(rows[SPAN - 1 :], ((0, SPAN - 1), (0, 0)))


def shift_down(rows):
    return jnp.pad(rows[: rows.shape[0] - SPAN + 1], ((SPAN - 1, 0), (0, 0)))


def body(
    hidden, query_weight, key_weight, value_weight, output_weight,
    encoded, location, neighbours, pattern, grad_out,
):
    ids = jnp.pad(neighbours + 256 * pattern, ((0, 0), (0, 126)))
    qg, rows, every_ids = fetch(
        shift_up(hidden), query_weight, encoded.reshape(512, 4096),
        key_weight, value_weight, shift_up(grad_out), output_weight, ids,
    )
    qg = qg.reshape(2, 32, SPAN, 512)
    rows = rows.reshape(8, 2, 4, NTOK, 512)
    stats = combine(stats_of(every_ids, location, qg, rows))
    og, grads = attend(every_ids, location, qg, rows, stats)
    attended, grad_hidden, grad_encoded = give_back(
        og.reshape(2, 4, 512, 512), grads, key_weight, value_weight, output_weight, query_weight
    )
    return shift_down(attended), shift_down(grad_hidden), grad_encoded.reshape(1, NTOK, 4096)


def solution(mesh):
    return jax.shard_map(
        body,
        mesh=mesh,
        in_specs=(
            P("dp", "head"),
            P("head", None),
            P(None, "head"),
            P(None, "head"),
            P(None, "head"),
            P("dp", None, None),
            P(),
            P("dp", None),
            P("dp", None),
            P("dp", "head"),
        ),
        out_specs=(P("dp", "head"), P("dp", "head"), P(("dp", "head"), None, None)),
        check_vma=False,
    )
```

```python
import functools

import jax
import jax.numpy as jnp
from jax import lax
from jax.experimental import pallas as pl
from jax.experimental.pallas import tpu as pltpu
from jax.sharding import PartitionSpec as P

HD = 128
SPAN = 64
NTOK = 128
MESH = pl.DeviceIdType.MESH
BF = jnp.bfloat16
F32 = jnp.float32
NEG = -1e30
SCALE = HD**-0.5
ANY = pl.BlockSpec(memory_space=pl.ANY)
VM = pl.BlockSpec(memory_space=pltpu.VMEM)
SM = pl.BlockSpec(memory_space=pltpu.SMEM)
CHUNKS = 4
TC = NTOK // CHUNKS
OUTPUT_UNITS = ((0, 0, 128), (0, 128, 128), (0, 256, 256), (1, 0, 256), (1, 256, 256))
QUERY_UNITS = tuple((w, first, 128) for w in range(2) for first in range(0, 512, 128))


def dot(a, b, ca, cb):
    return lax.dot_general(a, b, (((ca,), (cb,)), ((), ())), preferred_element_type=F32)


class Ring:
    def __init__(self, me, place):
        self.me = me
        self.p = me + 1 - 2 * (me % 2)
        self.q = 3 - me
        self.far = (me + 2) % 4
        self.dev_p = place(self.p)
        self.dev_q = place(self.q)
        self.dev_far = place(self.far)


def rings():
    dp = lax.axis_index("dp")
    x = lax.axis_index("head")
    z, y, c = dp // 8, (dp // 2) % 4, dp % 2
    ring_z = Ring(z, lambda v: ((v * 4 + y) * 2 + c, x))
    ring_y = Ring(y, lambda v: ((z * 4 + v) * 2 + c, x))
    ring_x = Ring(x, lambda v: (dp, v))
    sister = ((z * 4 + y) * 2 + 1 - c, x)
    return ring_z, ring_y, ring_x, sister, c


def greet(devices):
    barrier = pltpu.get_barrier_semaphore()
    for device in devices:
        pl.semaphore_signal(barrier, inc=1, device_id=device, device_id_type=MESH)
    pl.semaphore_wait(barrier, len(devices))


class Copies:
    def __init__(self, send, recv, local):
        self.send, self.recv, self.local = send, recv, local
        self.remote_count = self.local_count = 0
        self.started = []

    def push(self, src, dst, device):
        index = self.remote_count
        self.remote_count += 1
        copy = pltpu.make_async_remote_copy(
            src_ref=src,
            dst_ref=dst,
            send_sem=self.send.at[index],
            recv_sem=self.recv.at[index],
            device_id=device,
            device_id_type=MESH,
        )
        copy.start()
        self.started.append(copy)
        return copy

    def move(self, src, dst):
        index = self.local_count
        self.local_count += 1
        copy = pltpu.make_async_copy(src, dst, self.local.at[index])
        copy.start()
        return copy

    def finish(self):
        for copy in self.started:
            copy.wait_send()


class Reduce:
    def __init__(self, copies, ring, part, tmp, got):
        self.copies, self.ring, self.part, self.tmp, self.got = copies, ring, part, tmp, got

    def start(self):
        r, part = self.ring, self.part
        self.to_far = (
            self.copies.push(part(r.far, 0), self.tmp(0), r.dev_p),
            self.copies.push(part(r.far, 1), self.tmp(1), r.dev_q),
        )
        self.near = (
            self.copies.push(part(r.p, 0), self.got(0), r.dev_p),
            self.copies.push(part(r.q, 1), self.got(3), r.dev_q),
        )

    def relay(self, add):
        r, part = self.ring, self.part
        self.to_far[0].wait_recv()
        add(part(r.q, 0), part(r.q, 0), self.tmp(0))
        first = self.copies.push(part(r.q, 0), self.got(2), r.dev_q)
        self.to_far[1].wait_recv()
        add(part(r.p, 1), part(r.p, 1), self.tmp(1))
        second = self.copies.push(part(r.p, 1), self.got(1), r.dev_p)
        self.near = self.near + (first, second)

    def end(self, add, own):
        for copy in self.near:
            copy.wait_recv()
        add(own(0), self.part(self.ring.me, 0), self.got(0), self.got(2))
        add(own(1), self.part(self.ring.me, 1), self.got(1), self.got(3))


class Gather:
    def __init__(self, copies, ring, slot):
        self.copies, self.ring, self.slot = copies, ring, slot

    def start(self, own):
        r = self.ring
        self.to_p = self.copies.push(own, self.slot(r.me), r.dev_p)
        self.to_q = self.copies.push(own, self.slot(r.me), r.dev_q)

    def relay_p(self):
        r = self.ring
        self.to_p.wait_recv()
        self.fwd_q = self.copies.push(self.slot(r.p, 0), self.slot(r.p, 0), r.dev_q)

    def relay_q(self):
        r = self.ring
        self.to_q.wait_recv()
        self.fwd_p = self.copies.push(self.slot(r.q, 1), self.slot(r.q, 1), r.dev_p)

    def relay(self):
        self.relay_p()
        self.relay_q()

    def end(self):
        self.fwd_q.wait_recv()
        self.fwd_p.wait_recv()


def add_up(terms):
    if len(terms) == 2:
        return terms[0] + terms[1]
    return sum(t.astype(F32) for t in terms).astype(BF)


def add_rows(out, *terms):
    if len(out.shape) == 3:
        for index in range(out.shape[0]):
            out[index] = add_up([t[index] for t in terms])
        return

    def block(i, carry):
        rows = pl.ds(pl.multiple_of(i * 32, 32), 32)
        out[rows] = add_up([t[rows] for t in terms])
        return carry

    lax.fori_loop(0, out.shape[0] // 32, block, 0)


def fetch_kernel(
    loc_ref, hid, wq, enc, wk, wv, gout, wo, ids,
    qg_out, rows_out, ids_out, stats_out,
    v_hid, v_wq, v_enc, v_wk, v_wv, v_gout, v_wo, part, tmp, got, shifted, qg, rows, ids_ref, stats, held,
    send, recv, local,
):
    ring_z, ring_y, ring_x, sister, c = rings()
    copies = Copies(send, recv, local)
    loads = [
        copies.move(a, b)
        for a, b in (
            (hid, v_hid), (wq, v_wq), (enc, v_enc), (wk, v_wk), (wv, v_wv), (gout, v_gout), (wo, v_wo),
        )
    ]
    greet(
        [ring_x.dev_p, ring_x.dev_q, ring_y.dev_p, ring_y.dev_q, ring_z.dev_p, ring_z.dev_q, ring_z.dev_far, sister]
    )
    id_copies = [
        copies.push(ids, ids_out.at[ring_z.me], d) for d in (ring_z.dev_p, ring_z.dev_q, ring_z.dev_far)
    ]
    own_ids = copies.move(ids, ids_out.at[ring_z.me])

    def unit_of(u):
        w, first, size = QUERY_UNITS[u]
        half_size = size // 2

        def rows_of(half):
            return pl.ds(first + half * half_size, half_size)

        reduce = Reduce(
            copies,
            ring_x,
            lambda i, half: part.at[w, i, rows_of(half)],
            lambda half: tmp.at[w, rows_of(half)],
            lambda k: got.at[w, k // 2, rows_of(k % 2)],
        )

        def slot(i, half=None):
            return qg.at[w, i, pl.ds(first, size) if half is None else rows_of(half)]

        return reduce, Gather(copies, ring_z, slot)

    units = [unit_of(u) for u in range(len(QUERY_UNITS))]

    def shift_tile(ref, t):
        first = min(t, 2) * 128
        row = lax.broadcasted_iota(jnp.int32, (128, 256), 0) + (t * 128 + SPAN - 1 - first)
        col = lax.broadcasted_iota(jnp.int32, (128, 256), 1)
        move = (row == col).astype(BF)
        shifted[pl.ds(t * 128, 128), :] = dot(move, ref[pl.ds(first, 256), :], 1, 0).astype(BF)

    def query_rows(first, size):
        def tile(g, carry):
            cols = pl.ds(pl.multiple_of(g * 512, 512), 512)
            here = pl.ds(first, size)
            part[0, g, here] = dot(shifted[here, :], v_wq[:, cols], 1, 0).astype(BF)
            return carry

        lax.fori_loop(0, 4, tile, 0)

    def begin(u):
        units[u][0].start()

    def relay(u):
        units[u][0].relay(add_rows)

    def reduced(u):
        reduce, gather = units[u]
        reduce.end(add_rows, lambda half: gather.slot(ring_z.me, half))
        gather.start(gather.slot(ring_z.me))

    def spread(u):
        units[u][1].relay()

    out_copies = []

    def complete(u):
        w, first, size = QUERY_UNITS[u]
        units[u][1].end()
        here = pl.ds(first, size)
        out_copies.append(copies.move(qg.at[w, :, here], qg_out.at[w, :, here]))

    streams = []

    def project(s, weight):
        mine = rows.at[ring_y.me * 2 + c, s]

        def tile(j, carry):
            cols = pl.ds(pl.multiple_of(j * 256, 256), 256)
            mine[:, :, cols] = dot(v_enc[...], weight[:, cols], 1, 0).astype(BF).reshape(4, NTOK, 256)
            return carry

        lax.fori_loop(0, 2, tile, 0)

        def slot(i, half=None):
            block = rows.at[i * 2 + c, s]
            return block if half is None else block.at[pl.ds((half + s) % 2 * 2, 2)]

        gather = Gather(copies, ring_y, slot)
        gather.start(mine)
        streams.append((gather, [copies.push(mine, mine, sister)]))

    def forward(s):
        gather, to_sister = streams[s]
        gather.relay_p()
        to_sister.append(copies.push(gather.slot(ring_y.p), gather.slot(ring_y.p), sister))
        gather.relay_q()
        to_sister.append(copies.push(gather.slot(ring_y.q), gather.slot(ring_y.q), sister))

    def forwarded(s):
        gather, to_sister = streams[s]
        gather.fwd_q.wait_recv()
        to_sister.append(copies.push(gather.slot(ring_y.far, 0), gather.slot(ring_y.far, 0), sister))
        gather.fwd_p.wait_recv()
        to_sister.append(copies.push(gather.slot(ring_y.far, 1), gather.slot(ring_y.far, 1), sister))

    def rows_complete(s):
        for copy in streams[s][1]:
            copy.wait_recv()
        out_copies.append(copies.move(rows.at[:, s], rows_out.at[:, s]))

    loads[0].wait()
    shift_tile(v_hid, 0)
    loads[1].wait()
    query_rows(0, 128)
    begin(0)
    for t in range(1, 4):
        shift_tile(v_hid, t)
    query_rows(128, 384)
    begin(1)
    relay(0)
    begin(2)
    loads[2].wait()
    loads[3].wait()
    project(0, v_wk)
    relay(1)
    begin(3)
    reduced(0)
    loads[4].wait()
    project(1, v_wv)
    relay(2)
    reduced(1)
    loads[5].wait()
    for t in range(4):
        shift_tile(v_gout, t)
    loads[6].wait()

    def grad_tile(g, carry):
        here = pl.ds(pl.multiple_of(g * 512, 512), 512)
        part[1, g] = dot(shifted[...], v_wo[here, :], 1, 1).astype(BF)
        return carry

    lax.fori_loop(0, 4, grad_tile, 0)
    begin(4)
    relay(3)
    begin(5)
    reduced(2)
    spread(0)
    relay(4)
    begin(6)
    reduced(3)
    spread(1)
    forward(0)
    relay(5)
    begin(7)
    reduced(4)
    spread(2)
    relay(6)
    reduced(5)
    spread(3)
    forward(1)
    for copy in id_copies:
        copy.wait_recv()
    own_ids.wait()
    copies.move(ids_out, ids_ref).wait()
    relay(7)
    reduced(6)
    spread(4)
    reduced(7)
    spread(5)
    forwarded(0)
    spread(6)
    forwarded(1)
    spread(7)
    for u in range(4):
        complete(u)
    rows_complete(0)
    rows_complete(1)
    plane = lax.axis_index("dp") // 8

    def stats_of_spans(first, n):
        def span(j, carry):
            i = j // n * 8 + first + j % n
            for pair in range(2):
                cols = pl.ds(pair * 256, 256)
                tokens = pl.ds(pl.multiple_of(i % 8 * SPAN, SPAN), SPAN)
                query = two_heads(qg[0, i // 8, tokens, cols])
                grad = two_heads(qg[1, i // 8, tokens, cols])
                made = []
                for k in range(2):
                    entry = ids_ref[i // 8, i % 8, k]
                    stored = loc_ref[entry % 256]
                    live = jnp.logical_and(entry >= 256, stored // 32 == plane).astype(F32)
                    row = stored % 32
                    key = rows[row // 4, 0, row % 4, :, cols]
                    value = rows[row // 4, 1, row % 4, :, cols]
                    score = dot(key, query, 1, 1) * SCALE
                    gw = dot(value, grad, 1, 1)
                    top = jnp.max(score, axis=0, keepdims=True)
                    e = jnp.exp(score - top)
                    total = jnp.sum(e, axis=0, keepdims=True) * live
                    inner = jnp.sum(e * gw, axis=0, keepdims=True) * live
                    made.append((top * live + NEG * (1.0 - live), total, inner))
                (top0, sum0, dot0), (top1, sum1, dot1) = made
                top = jnp.maximum(top0, top1)
                f0, f1 = jnp.exp(top0 - top), jnp.exp(top1 - top)
                line = pl.ds(i * 2 + pair, 1)
                stats[0, line, :] = top
                stats[1, line, :] = sum0 * f0 + sum1 * f1
                stats[2, line, :] = dot0 * f0 + dot1 * f1
            return carry

        lax.fori_loop(0, 4 * n, span, 0)

    for u in range(4):
        complete(4 + u)
        stats_of_spans(2 * u, 2)

    def stats_slot(i, half=None):
        return held.at[i] if half is None else held.at[i, :, pl.ds(half * 32, 32)]

    exchange = Gather(copies, ring_z, stats_slot)
    exchange.start(stats)
    held[ring_z.me] = stats[...]
    exchange.relay()
    exchange.end()
    tops = [held[k, 0] for k in range(4)]
    top = jnp.maximum(jnp.maximum(tops[0], tops[1]), jnp.maximum(tops[2], tops[3]))
    fades = [jnp.exp(t - top) for t in tops]
    total = sum(fades[k] * held[k, 1] for k in range(4))
    inner = sum(fades[k] * held[k, 2] for k in range(4))
    stats_out[0] = top
    stats_out[1] = 1.0 / total
    stats_out[2] = inner / total
    for copy in out_copies:
        copy.wait()
    copies.finish()


def fetch(loc, hid, wq, enc, wk, wv, gout, wo, ids):
    return pl.pallas_call(
        fetch_kernel,
        out_shape=[
            jax.ShapeDtypeStruct((2, 4, 512, 512), BF),
            jax.ShapeDtypeStruct((8, 2, 4, NTOK, 512), BF),
            jax.ShapeDtypeStruct((4, 8, 128), jnp.int32),
            jax.ShapeDtypeStruct((3, 64, 128), F32),
        ],
        in_specs=[SM] + [ANY] * 8,
        out_specs=[ANY] * 3 + [VM],
        scratch_shapes=[
            pltpu.VMEM((512, 1024), BF),
            pltpu.VMEM((1024, 2048), BF),
            pltpu.VMEM((512, 4096), BF),
            pltpu.VMEM((4096, 512), BF),
            pltpu.VMEM((4096, 512), BF),
            pltpu.VMEM((512, 1024), BF),
            pltpu.VMEM((2048, 1024), BF),
            pltpu.VMEM((2, 4, 512, 512), BF),
            pltpu.VMEM((2, 512, 512), BF),
            pltpu.VMEM((2, 2, 512, 512), BF),
            pltpu.VMEM((512, 1024), BF),
            pltpu.VMEM((2, 4, 512, 512), BF),
            pltpu.VMEM((8, 2, 4, NTOK, 512), BF),
            pltpu.SMEM((4, 8, 128), jnp.int32),
            pltpu.VMEM((3, 64, 128), F32),
            pltpu.VMEM((4, 3, 64, 128), F32),
            pltpu.SemaphoreType.DMA((112,)),
            pltpu.SemaphoreType.DMA((112,)),
            pltpu.SemaphoreType.DMA((32,)),
        ],
        compiler_params=pltpu.CompilerParams(
            collective_id=0, has_side_effects=True, vmem_limit_bytes=54 << 20
        ),
        name="project_and_gather",
    )(loc, hid, wq, enc, wk, wv, gout, wo, ids)


def list_live(ids_ref, loc_ref, live_ref):
    z = lax.axis_index("dp") // 8

    def one(i, count):
        entry = ids_ref[i // 16, (i // 2) % 8, i % 2]
        stored = loc_ref[entry % 256]
        live_ref[count] = (i // 2) * 32 + stored % 32
        live = jnp.logical_and(entry >= 256, stored // 32 == z)
        return count + live.astype(jnp.int32)

    return lax.fori_loop(0, 64, one, 0)


def pairs_of_slots(live_ref, count, work):
    def step(j, carry):
        first = live_ref[2 * j]
        both = 2 * j + 1 < count
        second = jnp.where(both, live_ref[2 * j + 1], first)
        work(
            (first // 32, first % 32, None),
            (second // 32, second % 32, both.astype(F32)),
        )
        return carry

    lax.fori_loop(0, (count + 1) // 2, step, 0)


def load_inputs(qg_ref, rows_ref, qg, rows, sems):
    moves = [pltpu.make_async_copy(qg_ref.at[w], qg.at[w], sems.at[w]) for w in range(2)]
    moves += [pltpu.make_async_copy(rows_ref.at[b], rows.at[b], sems.at[2 + b]) for b in range(8)]
    for move in moves:
        move.start()
    return moves


def two_heads(block):
    zero = jnp.zeros((SPAN, HD), BF)
    return jnp.concatenate(
        [
            jnp.concatenate([block[:, :HD], zero], axis=1),
            jnp.concatenate([zero, block[:, HD:]], axis=1),
        ],
        axis=0,
    )


LOCAL_SCRATCH = [
    pltpu.VMEM((2, 32, SPAN, 512), BF),
    pltpu.VMEM((8, 2, 4, NTOK, 512), BF),
    pltpu.SemaphoreType.DMA((10,)),
    pltpu.SMEM((65,), jnp.int32),
]


def attend_kernel(ids_ref, loc_ref, qg_ref, rows_ref, stats_ref, og_ref, grads_ref, qg, rows, sems, live_ref):
    moves = load_inputs(qg_ref, rows_ref, qg, rows, sems)
    count = list_live(ids_ref, loc_ref, live_ref)

    def clear(i, carry):
        for s in range(2):
            for r in range(4):
                grads_ref[i, s, r] = jnp.zeros((NTOK, 512), BF)
                og_ref[s, i * 4 + r] = jnp.zeros((SPAN, 512), BF)
        return carry

    lax.fori_loop(0, 8, clear, 0)
    for move in moves:
        move.wait()

    def work(*slots):
        made = []
        for i, row, weight in slots:
            for pair in range(2):
                cols = pl.ds(pair * 256, 256)
                key = rows[row // 4, 0, row % 4, :, cols]
                value = rows[row // 4, 1, row % 4, :, cols]
                query = two_heads(qg[0, i, :, cols])
                grad = two_heads(qg[1, i, :, cols])
                line = pl.ds(i * 2 + pair, 1)
                s = dot(key, query, 1, 1) * SCALE
                gw = dot(value, grad, 1, 1)
                share = stats_ref[1, line, :]
                if weight is not None:
                    share = share * weight
                w = jnp.exp(s - stats_ref[0, line, :]) * share
                ds = (w * (gw - stats_ref[2, line, :]) * SCALE).astype(BF)
                w = w.astype(BF)
                for which, probs, memory, other in ((0, w, value, grad), (1, ds, key, query)):
                    made.append((i, row, pair, which, dot(probs, memory, 0, 0), dot(probs, other, 1, 0)))
        for i, row, pair, which, out, slope in made:
            for h in range(2):
                head = pl.ds(pair * 256 + h * HD, HD)
                part = out[h * SPAN : (h + 1) * SPAN, h * HD : (h + 1) * HD]
                og_ref[which, i, :, head] = (og_ref[which, i, :, head].astype(F32) + part).astype(BF)
            cols = pl.ds(pair * 256, 256)
            grads_ref[row // 4, 1 - which, row % 4, :, cols] = (
                grads_ref[row // 4, 1 - which, row % 4, :, cols].astype(F32) + slope
            ).astype(BF)

    pairs_of_slots(live_ref, count, work)


def attend(ids, loc, qg, rows, stats):
    return pl.pallas_call(
        attend_kernel,
        out_shape=[
            jax.ShapeDtypeStruct((2, 32, SPAN, 512), BF),
            jax.ShapeDtypeStruct((8, 2, 4, NTOK, 512), BF),
        ],
        in_specs=[SM, SM, ANY, ANY, VM],
        out_specs=[VM, VM],
        scratch_shapes=LOCAL_SCRATCH,
        compiler_params=pltpu.CompilerParams(vmem_limit_bytes=52 << 20),
        name="attend_both_ways",
    )(ids, loc, qg, rows, stats)


def return_kernel(
    og_part, grads, wk, wv, wo, wq,
    attended, grad_hidden, grad_encoded,
    v_wk, v_wv, v_wo, v_wq, og, z_tmp, z_got, own, everyone, rg, c_got, y_tmp, y_got, mine, term, x_tmp, x_got,
    send, recv, local,
):
    ring_z, ring_y, ring_x, sister, c = rings()
    copies = Copies(send, recv, local)
    og_loads = [copies.move(og_part.at[w], og.at[w]) for w in range(2)]
    order = (ring_y.far, ring_y.p, ring_y.q, ring_y.me)
    rg_loads = [
        [
            copies.move(grads.at[i * 2 + c, :, :, pl.ds(t * TC, TC)], rg.at[i, :, :, pl.ds(t * TC, TC)])
            for i in order
        ]
        for t in range(CHUNKS)
    ]
    weight_loads = [copies.move(a, b) for a, b in ((wk, v_wk), (wv, v_wv), (wo, v_wo), (wq, v_wq))]
    greet([ring_x.dev_p, ring_x.dev_q, ring_y.dev_p, ring_y.dev_q, ring_z.dev_p, ring_z.dev_q, sister])
    swaps = [
        [
            copies.push(
                grads.at[i * 2 + 1 - c, :, :, pl.ds(t * TC, TC)],
                c_got.at[i, :, :, pl.ds(t * TC, TC)],
                sister,
            )
            for i in order
        ]
        for t in range(CHUNKS)
    ]

    def z_unit(u):
        w, first, size = OUTPUT_UNITS[u]
        half_size = size // 2

        def rows_of(half):
            return pl.ds(first + half * half_size, half_size)

        whole = pl.ds(first, size)
        reduce = Reduce(
            copies,
            ring_z,
            lambda i, half: og.at[w, i, rows_of(half)],
            lambda half: z_tmp.at[w, rows_of(half)],
            lambda k: z_got.at[w, k // 2, rows_of(k % 2)],
        )
        gather = Gather(
            copies, ring_x, lambda i, half=None: everyone.at[w, i, whole if half is None else rows_of(half)]
        )

        def done():
            reduce.end(add_rows, lambda half: own.at[w, rows_of(half)])
            gather.start(own.at[w, whole])
            everyone[w, ring_x.me, whole] = own[w, whole]

        return reduce, gather, done

    def y_unit(t):
        rows = pl.ds(t * TC, TC)
        by_row = Reduce(
            copies,
            ring_y,
            lambda i, half: rg.at[i, half, :, rows],
            lambda half: y_tmp.at[half, :, rows],
            lambda k: y_got.at[k, :, rows],
        )
        by_group = Reduce(
            copies,
            ring_x,
            lambda i, half: term.at[i, rows, pl.ds(half * 2048, 2048)],
            lambda half: x_tmp.at[half, rows],
            lambda k: x_got.at[k, rows],
        )
        return by_row, by_group

    z_units = [z_unit(u) for u in range(len(OUTPUT_UNITS))]
    y_units = [y_unit(t) for t in range(CHUNKS)]

    def y_start(t):
        rows = pl.ds(t * TC, TC)
        for k, i in enumerate(order):
            rg_loads[t][k].wait()
            swaps[t][k].wait_recv()
            for half in range(2):
                block = rg.at[i, half, :, rows]
                add_rows(block, block, c_got.at[i, half, :, rows])
        y_units[t][0].start()

    def y_done(t):
        rows = pl.ds(t * TC, TC)
        y_units[t][0].end(add_rows, lambda half: mine.at[half, :, rows])
        if t == 0:
            weight_loads[0].wait()
            weight_loads[1].wait()

        def tile(j, carry):
            cols = pl.ds(pl.multiple_of(j * 512, 512), 512)
            keys = mine[0, :, rows, :].reshape(4 * TC, 512)
            values = mine[1, :, rows, :].reshape(4 * TC, 512)
            product = dot(keys, v_wk[cols, :], 1, 1) + dot(values, v_wv[cols, :], 1, 1)
            term[:, rows, cols] = product.astype(BF).reshape(4, TC, 512)
            return carry

        lax.fori_loop(0, 8, tile, 0)
        y_units[t][1].start()

    def z_begin(u):
        z_units[u][0].start()

    def z_relay(u):
        z_units[u][0].relay(add_rows)

    def z_done(u):
        z_units[u][2]()

    def spread(u):
        z_units[u][1].relay()

    def y_relay(t):
        y_units[t][0].relay(add_rows)

    def x_relay(t):
        y_units[t][1].relay(add_rows)

    og_loads[0].wait()
    z_begin(0)
    z_begin(1)
    z_relay(0)
    y_start(0)
    z_begin(2)
    z_done(0)
    z_relay(1)
    y_start(1)
    y_relay(0)
    og_loads[1].wait()
    z_begin(3)
    z_done(1)
    spread(0)
    y_done(0)
    z_relay(2)
    y_start(2)
    y_relay(1)
    spread(1)
    z_done(2)
    z_begin(4)
    x_relay(0)
    y_done(1)
    z_relay(3)
    y_start(3)
    y_relay(2)
    spread(2)
    z_done(3)
    x_relay(1)
    y_done(2)
    z_relay(4)
    y_relay(3)
    spread(3)
    z_done(4)
    x_relay(2)
    y_done(3)
    spread(4)
    x_relay(3)

    weight_loads[2].wait()
    weight_loads[3].wait()

    def result(t):
        rows = pl.ds(t * TC, TC)
        y_units[t][1].end(add_rows, lambda half: grad_encoded.at[rows, pl.ds(half * 2048, 2048)])

    def attended_tile(j, carry):
        cols = pl.ds(pl.multiple_of(j * 256, 256), 256)
        total = dot(everyone[0, 0], v_wo[0:512, cols], 1, 0)
        for g in range(1, 4):
            total = total + dot(everyone[0, g], v_wo[g * 512 : (g + 1) * 512, cols], 1, 0)
        attended[:, cols] = total.astype(BF)
        return carry

    def hidden_rows(first):
        rows = pl.ds(first, 256)

        def tile(j, carry):
            cols = pl.ds(pl.multiple_of(j * 256, 256), 256)
            total = dot(everyone[1, 0, rows], v_wq[cols, 0:512], 1, 1)
            for g in range(1, 4):
                total = total + dot(everyone[1, g, rows], v_wq[cols, g * 512 : (g + 1) * 512], 1, 1)
            grad_hidden[rows, cols] = total.astype(BF)
            return carry

        lax.fori_loop(0, 4, tile, 0)

    for u in range(3):
        z_units[u][1].end()
    lax.fori_loop(0, 4, attended_tile, 0)
    result(0)
    result(1)
    result(2)
    z_units[3][1].end()
    hidden_rows(0)
    z_units[4][1].end()
    hidden_rows(256)
    result(3)
    copies.finish()


def give_back(og_part, grads, wk, wv, wo, wq):
    return pl.pallas_call(
        return_kernel,
        out_shape=[
            jax.ShapeDtypeStruct((512, 1024), BF),
            jax.ShapeDtypeStruct((512, 1024), BF),
            jax.ShapeDtypeStruct((NTOK, 4096), BF),
        ],
        in_specs=[ANY] * 6,
        out_specs=[VM] * 3,
        scratch_shapes=[
            pltpu.VMEM((4096, 512), BF),
            pltpu.VMEM((4096, 512), BF),
            pltpu.VMEM((2048, 1024), BF),
            pltpu.VMEM((1024, 2048), BF),
            pltpu.VMEM((2, 4, 512, 512), BF),
            pltpu.VMEM((2, 512, 512), BF),
            pltpu.VMEM((2, 2, 512, 512), BF),
            pltpu.VMEM((2, 512, 512), BF),
            pltpu.VMEM((2, 4, 512, 512), BF),
            pltpu.VMEM((4, 2, 4, NTOK, 512), BF),
            pltpu.VMEM((4, 2, 4, NTOK, 512), BF),
            pltpu.VMEM((2, 4, NTOK, 512), BF),
            pltpu.VMEM((4, 4, NTOK, 512), BF),
            pltpu.VMEM((2, 4, NTOK, 512), BF),
            pltpu.VMEM((4, NTOK, 4096), BF),
            pltpu.VMEM((2, NTOK, 2048), BF),
            pltpu.VMEM((4, NTOK, 2048), BF),
            pltpu.SemaphoreType.DMA((128,)),
            pltpu.SemaphoreType.DMA((128,)),
            pltpu.SemaphoreType.DMA((32,)),
        ],
        compiler_params=pltpu.CompilerParams(
            collective_id=1, has_side_effects=True, vmem_limit_bytes=60 << 20
        ),
        name="reduce_and_project",
    )(og_part, grads, wk, wv, wo, wq)


def shift_down(rows):
    return jnp.pad(rows[: rows.shape[0] - SPAN + 1], ((SPAN - 1, 0), (0, 0)))


def body(
    hidden, query_weight, key_weight, value_weight, output_weight,
    encoded, location, neighbours, pattern, grad_out,
):
    ids = jnp.pad(neighbours + 256 * pattern, ((0, 0), (0, 126)))
    qg, rows, every_ids, stats = fetch(
        location, hidden, query_weight, encoded.reshape(512, 4096),
        key_weight, value_weight, grad_out, output_weight, ids,
    )
    qg = qg.reshape(2, 32, SPAN, 512)
    og, grads = attend(every_ids, location, qg, rows, stats)
    attended, grad_hidden, grad_encoded = give_back(
        og.reshape(2, 4, 512, 512), grads, key_weight, value_weight, output_weight, query_weight
    )
    return shift_down(attended), shift_down(grad_hidden), grad_encoded.reshape(1, NTOK, 4096)


def solution(mesh):
    return jax.shard_map(
        body,
        mesh=mesh,
        in_specs=(
            P("dp", "head"),
            P("head", None),
            P(None, "head"),
            P(None, "head"),
            P(None, "head"),
            P("dp", None, None),
            P(),
            P("dp", None),
            P("dp", None),
            P("dp", "head"),
        ),
        out_specs=(P("dp", "head"), P("dp", "head"), P(("dp", "head"), None, None)),
        check_vma=False,
    )
```

```python
import functools

import jax
import jax.numpy as jnp
from jax import lax
from jax.experimental import pallas as pl
from jax.experimental.pallas import tpu as pltpu
from jax.sharding import PartitionSpec as P

HD = 128
SPAN = 64
NTOK = 128
MESH = pl.DeviceIdType.MESH
BF = jnp.bfloat16
F32 = jnp.float32
NEG = -1e30
SCALE = HD**-0.5
ANY = pl.BlockSpec(memory_space=pl.ANY)
VM = pl.BlockSpec(memory_space=pltpu.VMEM)
SM = pl.BlockSpec(memory_space=pltpu.SMEM)
CHUNKS = 4
TC = NTOK // CHUNKS
SPANS = 8


def dot(a, b, ca, cb):
    return lax.dot_general(a, b, (((ca,), (cb,)), ((), ())), preferred_element_type=F32)


class Ring:
    def __init__(self, me, place):
        self.me = me
        self.p = me + 1 - 2 * (me % 2)
        self.q = 3 - me
        self.far = (me + 2) % 4
        self.dev_p = place(self.p)
        self.dev_q = place(self.q)
        self.dev_far = place(self.far)


def rings():
    dp = lax.axis_index("dp")
    x = lax.axis_index("head")
    z, y, c = dp // 8, (dp // 2) % 4, dp % 2
    ring_z = Ring(z, lambda v: ((v * 4 + y) * 2 + c, x))
    ring_y = Ring(y, lambda v: ((z * 4 + v) * 2 + c, x))
    ring_x = Ring(x, lambda v: (dp, v))
    sister = ((z * 4 + y) * 2 + 1 - c, x)
    return ring_z, ring_y, ring_x, sister, c


def greet(devices):
    barrier = pltpu.get_barrier_semaphore()
    for device in devices:
        pl.semaphore_signal(barrier, inc=1, device_id=device, device_id_type=MESH)
    pl.semaphore_wait(barrier, len(devices))


class Copies:
    def __init__(self, send, recv, local):
        self.send, self.recv, self.local = send, recv, local
        self.remote_count = self.local_count = 0
        self.started = []

    def push(self, src, dst, device):
        index = self.remote_count
        self.remote_count += 1
        copy = pltpu.make_async_remote_copy(
            src_ref=src,
            dst_ref=dst,
            send_sem=self.send.at[index],
            recv_sem=self.recv.at[index],
            device_id=device,
            device_id_type=MESH,
        )
        copy.start()
        self.started.append(copy)
        return copy

    def move(self, src, dst):
        index = self.local_count
        self.local_count += 1
        copy = pltpu.make_async_copy(src, dst, self.local.at[index])
        copy.start()
        return copy

    def finish(self):
        for copy in self.started:
            copy.wait_send()
        self.started = []


class Reduce:
    def __init__(self, copies, ring, part, tmp, got):
        self.copies, self.ring, self.part, self.tmp, self.got = copies, ring, part, tmp, got

    def start(self):
        r, part = self.ring, self.part
        self.to_far = (
            self.copies.push(part(r.far, 0), self.tmp(0), r.dev_p),
            self.copies.push(part(r.far, 1), self.tmp(1), r.dev_q),
        )
        self.near = (
            self.copies.push(part(r.p, 0), self.got(0), r.dev_p),
            self.copies.push(part(r.q, 1), self.got(3), r.dev_q),
        )

    def relay(self, add):
        r, part = self.ring, self.part
        self.to_far[0].wait_recv()
        add(part(r.q, 0), part(r.q, 0), self.tmp(0))
        first = self.copies.push(part(r.q, 0), self.got(2), r.dev_q)
        self.to_far[1].wait_recv()
        add(part(r.p, 1), part(r.p, 1), self.tmp(1))
        second = self.copies.push(part(r.p, 1), self.got(1), r.dev_p)
        self.near = self.near + (first, second)

    def end(self, add, own):
        for copy in self.near:
            copy.wait_recv()
        add(own(0), self.part(self.ring.me, 0), self.got(0), self.got(2))
        add(own(1), self.part(self.ring.me, 1), self.got(1), self.got(3))


class Gather:
    def __init__(self, copies, ring, slot):
        self.copies, self.ring, self.slot = copies, ring, slot

    def start(self, own):
        r = self.ring
        self.to_p = self.copies.push(own, self.slot(r.me), r.dev_p)
        self.to_q = self.copies.push(own, self.slot(r.me), r.dev_q)

    def relay_p(self):
        r = self.ring
        self.to_p.wait_recv()
        self.fwd_q = self.copies.push(self.slot(r.p, 0), self.slot(r.p, 0), r.dev_q)

    def relay_q(self):
        r = self.ring
        self.to_q.wait_recv()
        self.fwd_p = self.copies.push(self.slot(r.q, 1), self.slot(r.q, 1), r.dev_p)

    def relay(self):
        self.relay_p()
        self.relay_q()

    def end(self):
        self.fwd_q.wait_recv()
        self.fwd_p.wait_recv()


def add_up(terms):
    if len(terms) == 2:
        return terms[0] + terms[1]
    return sum(t.astype(F32) for t in terms).astype(BF)


def add_rows(out, *terms):
    if len(out.shape) == 3:
        for index in range(out.shape[0]):
            out[index] = add_up([t[index] for t in terms])
    else:
        out[...] = add_up([t[...] for t in terms])


def kernel(
    loc_ref, hid, wq, enc, wk, wv, gout, wo, ids,
    attended, grad_hidden, grad_encoded, ids_out,
    v_hid, v_gout, shifted, wide, v_wk, v_wv, v_enc, part, tmp, got, qg, rows,
    ids_ref, stored_ref, table_ref, stats, held,
    c_got, y_tmp, y_got, mine, x_tmp, x_got, send, recv, local,
):
    ring_z, ring_y, ring_x, sister, c = rings()
    copies = Copies(send, recv, local)
    plane = lax.axis_index("dp") // 8

    def load_wide(which):
        if which == 0:
            return [copies.move(wq.at[:, :, pl.ds(g * 512, 512)], wide.at[pl.ds(g * 8, 8)]) for g in range(4)]
        return [copies.move(wo.at[:, :, pl.ds(j * 512, 512)], wide.at[pl.ds(32 + j * 16, 16)]) for j in range(2)]

    load_hid = copies.move(hid, v_hid)
    load_wq = load_wide(0)
    load_enc = [
        copies.move(enc.at[:, :, pl.ds(j * 512, 512)], v_enc.at[j // 4, j % 4]) for j in range(8)
    ]
    load_wk = copies.move(wk, v_wk)
    load_wv = copies.move(wv, v_wv)
    load_gout = copies.move(gout, v_gout)
    load_wo = load_wide(1)
    greet(
        [ring_x.dev_p, ring_x.dev_q, ring_y.dev_p, ring_y.dev_q, ring_z.dev_p, ring_z.dev_q, ring_z.dev_far, sister]
    )
    id_copies = [
        copies.push(ids, ids_out.at[ring_z.me], d) for d in (ring_z.dev_p, ring_z.dev_q, ring_z.dev_far)
    ]
    own_ids = copies.move(ids, ids_out.at[ring_z.me])


    def unit_of(w, u):
        reduce = Reduce(
            copies,
            ring_x,
            lambda i, half: part.at[w, i, 2 * u + half],
            lambda half: tmp.at[w, 2 * u + half],
            lambda k: got.at[w, k // 2, 2 * u + k % 2],
        )

        def slot(i, half=None):
            return qg.at[w, i, pl.ds(2 * u, 2)] if half is None else qg.at[w, i, 2 * u + half]

        return reduce, Gather(copies, ring_z, slot)

    units = [unit_of(n // 4, n % 4) for n in range(8)]

    def shift_tile(ref, t):
        first = min(t, 2) * 128
        row = lax.broadcasted_iota(jnp.int32, (128, 256), 0) + (t * 128 + SPAN - 1 - first)
        col = lax.broadcasted_iota(jnp.int32, (128, 256), 1)
        move = (row == col).astype(BF)
        shifted[pl.ds(t * 128, 128), :] = dot(move, ref[pl.ds(first, 256), :], 1, 0).astype(BF)

    def query_rows(first, size):
        def tile(g, carry):
            here = pl.ds(first, size)
            weight = wide[pl.ds(pl.multiple_of(g * 8, 8), 8)].reshape(1024, 512)
            product = dot(shifted[here, :], weight, 1, 0).astype(BF)
            part[0, g, pl.ds(first // SPAN, size // SPAN)] = product.reshape(size // SPAN, SPAN, 512)
            return carry

        lax.fori_loop(0, 4, tile, 0)

    def output_block(g, j):
        return wide[pl.ds(32 + j * 16 + g * 4, 4)].reshape(512, 512)

    def begin(n):
        units[n][0].start()

    def relay(n):
        units[n][0].relay(add_rows)

    def reduced(n):
        reduce, gather = units[n]
        reduce.end(add_rows, lambda half: gather.slot(ring_z.me, half))
        gather.start(gather.slot(ring_z.me))

    def spread(n):
        units[n][1].relay()


    streams = []

    def project(s, weight):
        own = rows.at[ring_y.me * 2 + c, s]

        def tile(j, carry):
            cols = pl.ds(pl.multiple_of(j * 256, 256), 256)
            total = dot(v_enc[0, 0].reshape(512, 512), weight[0:512, cols], 1, 0)
            for k in range(1, 8):
                block = v_enc[k // 4, k % 4].reshape(512, 512)
                total = total + dot(block, weight[k * 512 : (k + 1) * 512, cols], 1, 0)
            own[:, :, cols] = total.astype(BF).reshape(4, NTOK, 256)
            return carry

        lax.fori_loop(0, 2, tile, 0)

        def slot(i, half=None):
            block = rows.at[i * 2 + c, s]
            return block if half is None else block.at[pl.ds((half + s) % 2 * 2, 2)]

        gather = Gather(copies, ring_y, slot)
        gather.start(own)
        streams.append((gather, [copies.push(own, own, sister)]))

    def forward(s):
        gather, to_sister = streams[s]
        gather.relay_p()
        to_sister.append(copies.push(gather.slot(ring_y.p), gather.slot(ring_y.p), sister))
        gather.relay_q()
        to_sister.append(copies.push(gather.slot(ring_y.q), gather.slot(ring_y.q), sister))

    def forwarded(s):
        gather, to_sister = streams[s]
        gather.fwd_q.wait_recv()
        to_sister.append(copies.push(gather.slot(ring_y.far, 0), gather.slot(ring_y.far, 0), sister))
        gather.fwd_p.wait_recv()
        to_sister.append(copies.push(gather.slot(ring_y.far, 1), gather.slot(ring_y.far, 1), sister))

    load_hid.wait()
    shift_tile(v_hid, 0)
    for load in load_wq:
        load.wait()
    query_rows(0, 128)
    begin(0)
    for t in range(1, 4):
        shift_tile(v_hid, t)
    query_rows(128, 384)
    begin(1)
    relay(0)
    begin(2)
    for load in load_enc:
        load.wait()
    load_wk.wait()
    project(0, v_wk)
    relay(1)
    begin(3)
    reduced(0)
    load_wv.wait()
    project(1, v_wv)
    relay(2)
    reduced(1)
    load_gout.wait()
    for t in range(4):
        shift_tile(v_gout, t)
    for load in load_wo:
        load.wait()

    def grad_tile(g, carry):
        total = dot(shifted[:, 0:512], output_block(g, 0), 1, 1)
        total = total + dot(shifted[:, 512:1024], output_block(g, 1), 1, 1)
        part[1, g] = total.astype(BF).reshape(SPANS, SPAN, 512)
        return carry

    lax.fori_loop(0, 4, grad_tile, 0)
    begin(4)
    relay(3)
    begin(5)
    reduced(2)
    spread(0)
    relay(4)
    begin(6)
    reduced(3)
    spread(1)
    forward(0)
    relay(5)
    begin(7)
    reduced(4)
    spread(2)
    relay(6)
    reduced(5)
    spread(3)
    forward(1)
    for copy in id_copies:
        copy.wait_recv()
    own_ids.wait()
    copies.move(ids_out, ids_ref).wait()


    def store_row(n, carry):
        entry = ids_ref[n // 16, n // 2 % 8, n % 2]
        live = (entry >= 256).astype(jnp.int32)
        stored_ref[n] = (loc_ref[entry % 256] + 1) * live - 1
        return carry

    lax.fori_loop(0, 64, store_row, 0)

    def list_slots(n, carry):
        block = n // 4 + plane * 8
        sequence = n % 4
        count = first = second = row = 0
        for e in range(16):
            stored = stored_ref[sequence * 16 + e]
            match = jnp.logical_and(stored >= 0, stored // 4 == block).astype(jnp.int32)
            one = match * (count == 0).astype(jnp.int32) if e else match
            two = match - one
            first, second = first + one * e, second + two * e
            row = row + one * (stored % 4)
            count = count + match
        table_ref[0, n] = first
        table_ref[1, n] = second
        table_ref[2, n] = count
        table_ref[3, n] = row
        return carry

    lax.fori_loop(0, 32, list_slots, 0)
    relay(7)
    reduced(6)
    spread(4)
    reduced(7)
    spread(5)
    forwarded(0)
    spread(6)
    forwarded(1)
    spread(7)
    for n in range(4):
        units[n][1].end()
    for _, to_sister in streams:
        for copy in to_sister:
            copy.wait_recv()

    def memory_of(n, cols):
        stored = stored_ref[n]
        live = jnp.logical_and(stored >= 0, stored // 32 == plane).astype(F32)
        row = (stored + 32) % 32
        return rows[row // 4, 0, row % 4, :, cols], rows[row // 4, 1, row % 4, :, cols], live

    def stats_of_spans(first):
        def span(j, carry):
            sequence, place = j // 2, first + j % 2
            i = sequence * 8 + place
            for pair in range(2):
                cols = pl.ds(pair * 256, 256)
                query = two_heads(qg[0, sequence, place, :, cols])
                grad = two_heads(qg[1, sequence, place, :, cols])
                made = []
                for k in range(2):
                    key, value, live = memory_of(i * 2 + k, cols)
                    score = dot(key, query, 1, 1) * SCALE
                    gw = dot(value, grad, 1, 1)
                    top = jnp.max(score, axis=0, keepdims=True)
                    e = jnp.exp(score - top)
                    total = jnp.sum(e, axis=0, keepdims=True) * live
                    inner = jnp.sum(e * gw, axis=0, keepdims=True) * live
                    made.append((top * live + NEG * (1.0 - live), total, inner))
                (top0, sum0, dot0), (top1, sum1, dot1) = made
                top = jnp.maximum(top0, top1)
                f0, f1 = jnp.exp(top0 - top), jnp.exp(top1 - top)
                line = pl.ds(i * 2 + pair, 1)
                stats[0, line, :] = top
                stats[1, line, :] = sum0 * f0 + sum1 * f1
                stats[2, line, :] = dot0 * f0 + dot1 * f1
            return carry

        lax.fori_loop(0, 8, span, 0)

    for u in range(4):
        units[4 + u][1].end()
        stats_of_spans(2 * u)

    def stats_slot(i, half=None):
        return held.at[i] if half is None else held.at[i, :, pl.ds(half * 32, 32)]

    exchange = Gather(copies, ring_z, stats_slot)
    exchange.start(stats)
    held[ring_z.me] = stats[...]
    exchange.relay()
    exchange.end()
    copies.finish()
    tops = [held[k, 0] for k in range(4)]
    top = jnp.maximum(jnp.maximum(tops[0], tops[1]), jnp.maximum(tops[2], tops[3]))
    fades = [jnp.exp(t - top) for t in tops]
    total = sum(fades[k] * held[k, 1] for k in range(4))
    inner = sum(fades[k] * held[k, 2] for k in range(4))
    stats[0] = top
    stats[1] = 1.0 / total
    stats[2] = inner / total


    def attend_spans(first):
        def span(j, carry):
            sequence, place = j // 2, first + j % 2
            i = sequence * 8 + place
            for pair in range(2):
                cols = pl.ds(pair * 256, 256)
                query = two_heads(qg[0, sequence, place, :, cols])
                grad = two_heads(qg[1, sequence, place, :, cols])
                line = pl.ds(i * 2 + pair, 1)
                keys, values, ws, dss = [], [], [], []
                for k in range(2):
                    key, value, live = memory_of(i * 2 + k, cols)
                    score = dot(key, query, 1, 1) * SCALE
                    gw = dot(value, grad, 1, 1)
                    share = stats[1, line, :] * live
                    w = jnp.exp(jnp.minimum(score - stats[0, line, :], 0.0)) * share
                    ds = (w * (gw - stats[2, line, :]) * SCALE).astype(BF)
                    w = w.astype(BF)
                    wide[i * 2 + k, :, pl.ds(pair * 128, 128)] = w
                    wide[i * 2 + k, :, pl.ds(256 + pair * 128, 128)] = ds
                    keys.append(key)
                    values.append(value)
                    ws.append(w)
                    dss.append(ds)
                for which, probs, memory in ((0, ws, values), (1, dss, keys)):
                    out = dot(jnp.concatenate(probs, axis=0), jnp.concatenate(memory, axis=0), 0, 0)
                    for h in range(2):
                        part[which, sequence, place, :, pl.ds(pair * 256 + h * HD, HD)] = out[
                            h * SPAN : (h + 1) * SPAN, h * HD : (h + 1) * HD
                        ].astype(BF)
            return carry

        lax.fori_loop(0, 8, span, 0)

    def row_grads(block):
        for pair in range(2):
            cols = pl.ds(pair * 256, 256)
            for kv in range(2):
                made = []
                for sequence in range(4):
                    n = block * 4 + sequence
                    first, second = table_ref[0, n], table_ref[1, n]
                    both = (table_ref[2, n] >= 2).astype(F32)
                    place = pl.ds((256 if kv == 0 else 0) + pair * 128, 128)
                    probs = jnp.concatenate(
                        [
                            wide[sequence * 16 + first, :, place],
                            wide[sequence * 16 + second, :, place] * both.astype(BF),
                        ],
                        axis=1,
                    )
                    other = jnp.concatenate(
                        [
                            two_heads(qg[kv, sequence, first // 2, :, cols]),
                            two_heads(qg[kv, sequence, second // 2, :, cols]),
                        ],
                        axis=0,
                    )
                    made.append(dot(probs, other, 1, 0).astype(BF))
                for r in range(4):
                    total = None
                    for sequence in range(4):
                        n = block * 4 + sequence
                        pick = jnp.logical_and(table_ref[2, n] >= 1, table_ref[3, n] == r)
                        term = made[sequence] * pick.astype(F32).astype(BF)
                        total = term if total is None else total + term
                    rows[block, kv, r, :, cols] = total


    def z_unit(w, u):
        reduce = Reduce(
            copies,
            ring_z,
            lambda i, half: part.at[w, i, 2 * u + half],
            lambda half: tmp.at[w, 2 * u + half],
            lambda k: got.at[w, k // 2, 2 * u + k % 2],
        )

        def slot(i, half=None):
            return v_enc.at[w, i, pl.ds(2 * u, 2)] if half is None else v_enc.at[w, i, 2 * u + half]

        return reduce, Gather(copies, ring_x, slot)

    outs = [[z_unit(w, u) for u in range(4)] for w in range(2)]

    def zb(w, u):
        outs[w][u][0].start()

    def zr(w, u):
        outs[w][u][0].relay(add_rows)

    def zd(w, u):
        reduce, gather = outs[w][u]
        reduce.end(add_rows, lambda half: gather.slot(ring_x.me, half))
        gather.start(gather.slot(ring_x.me))

    def zs(w, u):
        outs[w][u][1].relay()


    order = (ring_y.far, ring_y.p, ring_y.q, ring_y.me)

    def y_unit(t):
        here = pl.ds(t * TC, TC)
        by_row = Reduce(
            copies,
            ring_y,
            lambda i, half: rows.at[i * 2 + c, half, :, here],
            lambda half: y_tmp.at[half, t],
            lambda k: y_got.at[k, t],
        )
        by_group = Reduce(
            copies,
            ring_x,
            lambda i, half: qg.at[half, :, i * 2 + t // 2, pl.ds(t % 2 * TC, TC)],
            lambda half: x_tmp.at[half, t],
            lambda k: x_got.at[k, t],
        )
        return by_row, by_group

    chunks = [y_unit(t) for t in range(CHUNKS)]
    swaps = []

    def sister_rows(k):
        block = order[k] * 2 + 1 - c
        row_grads(block)
        swaps.append(copies.push(rows.at[block], c_got.at[order[k]], sister))

    def own_rows(k):
        row_grads(order[k] * 2 + c)

    def y_start(t):
        here = pl.ds(t * TC, TC)
        for k, i in enumerate(order):
            if t == 0:
                swaps[k].wait_recv()
            for half in range(2):
                block = rows.at[i * 2 + c, half, :, here]
                add_rows(block, block, c_got.at[i, half, :, here])
        chunks[t][0].start()

    def y_relay(t):
        chunks[t][0].relay(add_rows)

    def y_done(t):
        chunks[t][0].end(add_rows, lambda half: mine.at[half])

        def tile(j, carry):
            cols = pl.ds(pl.multiple_of(j * 512, 512), 512)
            keys = mine[0].reshape(4 * TC, 512)
            values = mine[1].reshape(4 * TC, 512)
            product = dot(keys, v_wk[cols, :], 1, 1) + dot(values, v_wv[cols, :], 1, 1)
            product = product.astype(BF)
            for r in range(4):
                qg[j // 4, j % 4, r * 2 + t // 2, pl.ds(t % 2 * TC, TC), :] = product[r * TC : (r + 1) * TC]
            return carry

        lax.fori_loop(0, 8, tile, 0)
        chunks[t][1].start()

    def x_relay(t):
        chunks[t][1].relay(add_rows)

    def result(t):
        chunks[t][1].end(
            add_rows, lambda half: grad_encoded.at[pl.ds(half * 4, 4), pl.ds(t * TC, TC)]
        )

    attend_spans(0)
    zb(0, 0)
    attend_spans(2)
    zr(0, 0)
    zb(1, 0)
    zb(0, 1)
    attend_spans(4)
    zd(0, 0)
    zr(1, 0)
    zr(0, 1)
    zb(1, 1)
    attend_spans(6)
    zd(1, 0)
    zd(0, 1)
    zb(0, 2)
    sister_rows(0)
    zr(1, 1)
    zb(1, 2)
    zs(0, 0)
    sister_rows(1)
    zd(1, 1)
    zs(1, 0)
    sister_rows(2)
    zr(0, 2)
    zb(0, 3)
    zs(0, 1)
    sister_rows(3)
    zd(0, 2)
    zr(1, 2)
    zb(1, 3)
    own_rows(0)
    own_rows(1)
    zd(1, 2)
    zs(1, 1)
    own_rows(2)
    own_rows(3)
    again = load_wide(0) + load_wide(1)
    zr(0, 3)
    y_start(0)
    y_start(1)
    zd(0, 3)
    zs(0, 2)
    zr(1, 3)
    y_relay(0)
    y_start(2)
    zd(1, 3)
    zs(1, 2)
    y_done(0)
    y_relay(1)
    y_start(3)
    zs(0, 3)
    y_done(1)
    x_relay(0)
    y_relay(2)
    zs(1, 3)
    y_done(2)
    x_relay(1)
    y_relay(3)
    x_relay(2)
    y_done(3)
    for load in again:
        load.wait()
    for u in range(4):
        outs[0][u][1].end()

    def everyone(w, g, first, size):
        return v_enc[w, g, pl.ds(first // SPAN, size // SPAN)].reshape(size, 512)

    def attended_tile(j, carry):
        cols = pl.ds(pl.multiple_of(j % 2 * 256, 256), 256)
        total = None
        for g in range(4):
            weight = wide[pl.ds(32 + j // 2 * 16 + g * 4, 4), :, cols].reshape(512, 256)
            term = dot(everyone(0, g, 0, 512), weight, 1, 0)
            total = term if total is None else total + term
        attended[:, pl.ds(pl.multiple_of(j * 256, 256), 256)] = total.astype(BF)
        return carry

    def hidden_rows(first):
        def tile(j, carry):
            total = None
            for g in range(4):
                weight = wide[pl.ds(g * 8 + j * 2, 2)].reshape(256, 512)
                term = dot(everyone(1, g, first, 256), weight, 1, 1)
                total = term if total is None else total + term
            grad_hidden[pl.ds(first, 256), pl.ds(pl.multiple_of(j * 256, 256), 256)] = total.astype(BF)
            return carry

        lax.fori_loop(0, 4, tile, 0)

    lax.fori_loop(0, 4, attended_tile, 0)
    x_relay(3)
    result(0)
    result(1)
    result(2)
    for u in range(2):
        outs[1][u][1].end()
    hidden_rows(0)
    for u in range(2, 4):
        outs[1][u][1].end()
    hidden_rows(256)
    result(3)
    copies.finish()


def cross_attention(loc, hid, wq, enc, wk, wv, gout, wo, ids):
    return pl.pallas_call(
        kernel,
        out_shape=[
            jax.ShapeDtypeStruct((512, 1024), BF),
            jax.ShapeDtypeStruct((512, 1024), BF),
            jax.ShapeDtypeStruct((8, NTOK, 512), BF),
            jax.ShapeDtypeStruct((4, 8, 128), jnp.int32),
        ],
        in_specs=[SM] + [ANY] * 8,
        out_specs=[VM, VM, VM, ANY],
        scratch_shapes=[
            pltpu.VMEM((512, 1024), BF),
            pltpu.VMEM((512, 1024), BF),
            pltpu.VMEM((512, 1024), BF),
            pltpu.VMEM((64, 128, 512), BF),
            pltpu.VMEM((4096, 512), BF),
            pltpu.VMEM((4096, 512), BF),
            pltpu.VMEM((2, 4, SPANS, SPAN, 512), BF),
            pltpu.VMEM((2, 4, SPANS, SPAN, 512), BF),
            pltpu.VMEM((2, SPANS, SPAN, 512), BF),
            pltpu.VMEM((2, 2, SPANS, SPAN, 512), BF),
            pltpu.VMEM((2, 4, SPANS, SPAN, 512), BF),
            pltpu.VMEM((8, 2, 4, NTOK, 512), BF),
            pltpu.SMEM((4, 8, 128), jnp.int32),
            pltpu.SMEM((64,), jnp.int32),
            pltpu.SMEM((4, 32), jnp.int32),
            pltpu.VMEM((3, 64, 128), F32),
            pltpu.VMEM((4, 3, 64, 128), F32),
            pltpu.VMEM((4, 2, 4, NTOK, 512), BF),
            pltpu.VMEM((2, CHUNKS, 4, TC, 512), BF),
            pltpu.VMEM((4, CHUNKS, 4, TC, 512), BF),
            pltpu.VMEM((2, 4, TC, 512), BF),
            pltpu.VMEM((2, CHUNKS, 4, TC, 512), BF),
            pltpu.VMEM((4, CHUNKS, 4, TC, 512), BF),
            pltpu.SemaphoreType.DMA((256,)),
            pltpu.SemaphoreType.DMA((256,)),
            pltpu.SemaphoreType.DMA((40,)),
        ],
        compiler_params=pltpu.CompilerParams(
            collective_id=0, has_side_effects=True, vmem_limit_bytes=62 << 20
        ),
        name="cross_attention",
    )(loc, hid, wq, enc, wk, wv, gout, wo, ids)


def two_heads(block):
    zero = jnp.zeros((SPAN, HD), BF)
    return jnp.concatenate(
        [
            jnp.concatenate([block[:, :HD], zero], axis=1),
            jnp.concatenate([zero, block[:, HD:]], axis=1),
        ],
        axis=0,
    )


def shift_down(rows):
    return jnp.pad(rows[: rows.shape[0] - SPAN + 1], ((SPAN - 1, 0), (0, 0)))


def body(
    hidden, query_weight, key_weight, value_weight, output_weight,
    encoded, location, neighbours, pattern, grad_out,
):
    ids = jnp.pad(neighbours + 256 * pattern, ((0, 0), (0, 126)))
    attended, grad_hidden, grad_encoded, _ = cross_attention(
        location, hidden, query_weight.reshape(8, 128, 2048), encoded.reshape(8, 64, 4096),
        key_weight, value_weight, grad_out, output_weight.reshape(16, 128, 1024), ids,
    )
    grad_encoded = jnp.transpose(grad_encoded, (1, 0, 2)).reshape(1, NTOK, 4096)
    return shift_down(attended), shift_down(grad_hidden), grad_encoded


def solution(mesh):
    return jax.shard_map(
        body,
        mesh=mesh,
        in_specs=(
            P("dp", "head"),
            P("head", None),
            P(None, "head"),
            P(None, "head"),
            P(None, "head"),
            P("dp", None, None),
            P(),
            P("dp", None),
            P("dp", None),
            P("dp", "head"),
        ),
        out_specs=(P("dp", "head"), P("dp", "head"), P(("dp", "head"), None, None)),
        check_vma=False,
    )
```

```python
import functools

import jax
import jax.numpy as jnp
from jax import lax
from jax.experimental import pallas as pl
from jax.experimental.pallas import tpu as pltpu
from jax.sharding import PartitionSpec as P

HD = 128
SPAN = 64
NTOK = 128
MESH = pl.DeviceIdType.MESH
BF = jnp.bfloat16
F32 = jnp.float32
NEG = -1e30
SCALE = HD**-0.5
ANY = pl.BlockSpec(memory_space=pl.ANY)
VM = pl.BlockSpec(memory_space=pltpu.VMEM)
SM = pl.BlockSpec(memory_space=pltpu.SMEM)
CHUNKS = 2
TC = NTOK // CHUNKS
SPANS = 8


def dot(a, b, ca, cb):
    return lax.dot_general(a, b, (((ca,), (cb,)), ((), ())), preferred_element_type=F32)


class Ring:
    def __init__(self, me, place):
        self.me = me
        self.p = me + 1 - 2 * (me % 2)
        self.q = 3 - me
        self.far = (me + 2) % 4
        self.dev_p = place(self.p)
        self.dev_q = place(self.q)
        self.dev_far = place(self.far)


def rings():
    dp = lax.axis_index("dp")
    x = lax.axis_index("head")
    z, y, c = dp // 8, (dp // 2) % 4, dp % 2
    ring_z = Ring(z, lambda v: ((v * 4 + y) * 2 + c, x))
    ring_y = Ring(y, lambda v: ((z * 4 + v) * 2 + c, x))
    ring_x = Ring(x, lambda v: (dp, v))
    sister = ((z * 4 + y) * 2 + 1 - c, x)
    return ring_z, ring_y, ring_x, sister, c


def greet(devices):
    barrier = pltpu.get_barrier_semaphore()
    for device in devices:
        pl.semaphore_signal(barrier, inc=1, device_id=device, device_id_type=MESH)
    pl.semaphore_wait(barrier, len(devices))


class Copies:
    def __init__(self, send, recv, local):
        self.send, self.recv, self.local = send, recv, local
        self.remote_count = self.local_count = 0
        self.started = {}

    def push(self, src, dst, device):
        index = self.remote_count
        self.remote_count += 1
        copy = pltpu.make_async_remote_copy(
            src_ref=src,
            dst_ref=dst,
            send_sem=self.send.at[index],
            recv_sem=self.recv.at[index],
            device_id=device,
            device_id_type=MESH,
        )
        copy.start()
        self.started[id(copy)] = copy
        return copy

    def move(self, src, dst):
        index = self.local_count
        self.local_count += 1
        copy = pltpu.make_async_copy(src, dst, self.local.at[index])
        copy.start()
        return copy

    def settle(self, copy):
        if self.started.pop(id(copy), None) is not None:
            copy.wait_send()

    def finish(self):
        for copy in list(self.started.values()):
            self.settle(copy)


class Reduce:
    def __init__(self, copies, ring, part, tmp, got):
        self.copies, self.ring, self.part, self.tmp, self.got = copies, ring, part, tmp, got

    def start(self):
        r, part = self.ring, self.part
        self.to_far = (
            self.copies.push(part(r.far, 0), self.tmp(0), r.dev_p),
            self.copies.push(part(r.far, 1), self.tmp(1), r.dev_q),
        )
        self.near = (
            self.copies.push(part(r.p, 0), self.got(0), r.dev_p),
            self.copies.push(part(r.q, 1), self.got(3), r.dev_q),
        )

    def sent(self):
        for copy in self.to_far + self.near:
            self.copies.settle(copy)

    def relay(self, add):
        r, part = self.ring, self.part
        self.to_far[0].wait_recv()
        add(part(r.q, 0), part(r.q, 0), self.tmp(0))
        first = self.copies.push(part(r.q, 0), self.got(2), r.dev_q)
        self.to_far[1].wait_recv()
        add(part(r.p, 1), part(r.p, 1), self.tmp(1))
        second = self.copies.push(part(r.p, 1), self.got(1), r.dev_p)
        self.near = self.near + (first, second)

    def end(self, add, own):
        for copy in self.near:
            copy.wait_recv()
        add(own(0), self.part(self.ring.me, 0), self.got(0), self.got(2))
        add(own(1), self.part(self.ring.me, 1), self.got(1), self.got(3))


class Gather:
    def __init__(self, copies, ring, slot):
        self.copies, self.ring, self.slot = copies, ring, slot

    def start(self, own):
        r = self.ring
        self.to_p = self.copies.push(own, self.slot(r.me), r.dev_p)
        self.to_q = self.copies.push(own, self.slot(r.me), r.dev_q)

    def relay_p(self):
        r = self.ring
        self.to_p.wait_recv()
        self.fwd_q = self.copies.push(self.slot(r.p, 0), self.slot(r.p, 0), r.dev_q)

    def relay_q(self):
        r = self.ring
        self.to_q.wait_recv()
        self.fwd_p = self.copies.push(self.slot(r.q, 1), self.slot(r.q, 1), r.dev_p)

    def relay(self):
        self.relay_p()
        self.relay_q()

    def end(self):
        self.fwd_q.wait_recv()
        self.fwd_p.wait_recv()


def add_up(terms):
    if len(terms) == 2:
        return terms[0] + terms[1]
    return sum(t.astype(F32) for t in terms).astype(BF)


def add_rows(out, *terms):
    if len(out.shape) == 3:
        for index in range(out.shape[0]):
            out[index] = add_up([t[index] for t in terms])
    else:
        out[...] = add_up([t[...] for t in terms])


def kernel(
    loc_ref, hid, wq, enc, wk, wv, gout, wo, ids,
    attended, grad_hidden, grad_encoded, ids_out,
    v_hid, v_gout, shifted, wide, v_wk, v_wv, v_enc, part, tmp, got, qg, rows,
    ids_ref, stored_ref, table_ref, stats, held,
    c_got, y_tmp, y_got, mine, x_tmp, x_got, send, recv, local,
):
    ring_z, ring_y, ring_x, sister, c = rings()
    copies = Copies(send, recv, local)
    plane = lax.axis_index("dp") // 8

    def load_wide(which):
        if which == 0:
            return [copies.move(wq.at[:, :, pl.ds(g * 512, 512)], wide.at[pl.ds(g * 8, 8)]) for g in range(4)]
        return [copies.move(wo.at[:, :, pl.ds(j * 512, 512)], wide.at[pl.ds(32 + j * 16, 16)]) for j in range(2)]

    load_hid = copies.move(hid, v_hid)
    load_wq = load_wide(0)
    load_enc = [
        copies.move(enc.at[:, :, pl.ds(j * 512, 512)], v_enc.at[j // 4, j % 4]) for j in range(8)
    ]
    load_wk = copies.move(wk, v_wk)
    load_wv = copies.move(wv, v_wv)
    load_gout = copies.move(gout, v_gout)
    load_wo = load_wide(1)
    greet(
        [ring_x.dev_p, ring_x.dev_q, ring_y.dev_p, ring_y.dev_q, ring_z.dev_p, ring_z.dev_q, ring_z.dev_far, sister]
    )
    id_copies = [
        copies.push(ids, ids_out.at[ring_z.me], d) for d in (ring_z.dev_p, ring_z.dev_q, ring_z.dev_far)
    ]
    own_ids = copies.move(ids, ids_out.at[ring_z.me])


    def unit_of(w, u):
        reduce = Reduce(
            copies,
            ring_x,
            lambda i, half: part.at[w, i, 2 * u + half],
            lambda half: tmp.at[w, 2 * u + half],
            lambda k: got.at[w, k // 2, 2 * u + k % 2],
        )

        def slot(i, half=None):
            return qg.at[w, i, pl.ds(2 * u, 2)] if half is None else qg.at[w, i, 2 * u + half]

        return reduce, Gather(copies, ring_z, slot)

    units = [unit_of(n // 4, n % 4) for n in range(8)]

    def shift_tile(ref, t):
        first = min(t, 2) * 128
        row = lax.broadcasted_iota(jnp.int32, (128, 256), 0) + (t * 128 + SPAN - 1 - first)
        col = lax.broadcasted_iota(jnp.int32, (128, 256), 1)
        move = (row == col).astype(BF)
        shifted[pl.ds(t * 128, 128), :] = dot(move, ref[pl.ds(first, 256), :], 1, 0).astype(BF)

    def query_rows(first, size):
        def tile(g, carry):
            here = pl.ds(first, size)
            weight = wide[pl.ds(pl.multiple_of(g * 8, 8), 8)].reshape(1024, 512)
            product = dot(shifted[here, :], weight, 1, 0).astype(BF)
            part[0, g, pl.ds(first // SPAN, size // SPAN)] = product.reshape(size // SPAN, SPAN, 512)
            return carry

        lax.fori_loop(0, 4, tile, 0)

    def output_block(g, j):
        return wide[pl.ds(32 + j * 16 + g * 4, 4)].reshape(512, 512)

    def begin(n):
        units[n][0].start()

    def relay(n):
        units[n][0].relay(add_rows)

    def reduced(n):
        reduce, gather = units[n]
        reduce.end(add_rows, lambda half: gather.slot(ring_z.me, half))
        gather.start(gather.slot(ring_z.me))

    def spread(n):
        units[n][1].relay()


    streams = []

    def project(s, weight):
        own = rows.at[ring_y.me * 2 + c, s]

        def tile(j, carry):
            cols = pl.ds(pl.multiple_of(j * 256, 256), 256)
            total = dot(v_enc[0, 0].reshape(512, 512), weight[0:512, cols], 1, 0)
            for k in range(1, 8):
                block = v_enc[k // 4, k % 4].reshape(512, 512)
                total = total + dot(block, weight[k * 512 : (k + 1) * 512, cols], 1, 0)
            own[:, :, cols] = total.astype(BF).reshape(4, NTOK, 256)
            return carry

        lax.fori_loop(0, 2, tile, 0)

        def slot(i, half=None):
            block = rows.at[i * 2 + c, s]
            return block if half is None else block.at[pl.ds((half + s) % 2 * 2, 2)]

        gather = Gather(copies, ring_y, slot)
        gather.start(own)
        streams.append((gather, [copies.push(own, own, sister)]))

    def forward(s):
        gather, to_sister = streams[s]
        gather.relay_p()
        to_sister.append(copies.push(gather.slot(ring_y.p), gather.slot(ring_y.p), sister))
        gather.relay_q()
        to_sister.append(copies.push(gather.slot(ring_y.q), gather.slot(ring_y.q), sister))

    def forwarded(s):
        gather, to_sister = streams[s]
        gather.fwd_q.wait_recv()
        to_sister.append(copies.push(gather.slot(ring_y.far, 0), gather.slot(ring_y.far, 0), sister))
        gather.fwd_p.wait_recv()
        to_sister.append(copies.push(gather.slot(ring_y.far, 1), gather.slot(ring_y.far, 1), sister))

    load_hid.wait()
    shift_tile(v_hid, 0)
    for load in load_wq:
        load.wait()
    query_rows(0, 128)
    begin(0)
    for load in load_enc:
        load.wait()
    load_wk.wait()
    project(0, v_wk)
    for t in range(1, 4):
        shift_tile(v_hid, t)
    query_rows(128, 384)
    begin(1)
    relay(0)
    begin(2)
    load_wv.wait()
    project(1, v_wv)
    relay(1)
    begin(3)
    reduced(0)
    load_gout.wait()
    for t in range(4):
        shift_tile(v_gout, t)
    for load in load_wo:
        load.wait()

    def grad_tile(g, carry):
        total = dot(shifted[:, 0:512], output_block(g, 0), 1, 1)
        total = total + dot(shifted[:, 512:1024], output_block(g, 1), 1, 1)
        part[1, g] = total.astype(BF).reshape(SPANS, SPAN, 512)
        return carry

    lax.fori_loop(0, 4, grad_tile, 0)
    relay(2)
    begin(4)
    reduced(1)
    spread(0)
    relay(3)
    begin(5)
    reduced(2)
    spread(1)
    forward(0)
    relay(4)
    begin(6)
    reduced(3)
    spread(2)
    relay(5)
    begin(7)
    reduced(4)
    spread(3)
    forward(1)
    for copy in id_copies:
        copy.wait_recv()
    own_ids.wait()
    copies.move(ids_out, ids_ref).wait()


    def store_row(n, carry):
        entry = ids_ref[n // 16, n // 2 % 8, n % 2]
        live = (entry >= 256).astype(jnp.int32)
        stored_ref[n] = (loc_ref[entry % 256] + 1) * live - 1
        return carry

    lax.fori_loop(0, 64, store_row, 0)

    def list_slots(n, carry):
        block = n // 4 + plane * 8
        sequence = n % 4
        count = first = second = row = 0
        for e in range(16):
            stored = stored_ref[sequence * 16 + e]
            match = jnp.logical_and(stored >= 0, stored // 4 == block).astype(jnp.int32)
            one = match * (count == 0).astype(jnp.int32) if e else match
            two = match - one
            first, second = first + one * e, second + two * e
            row = row + one * (stored % 4)
            count = count + match
        table_ref[0, n] = first
        table_ref[1, n] = second
        table_ref[2, n] = count
        table_ref[3, n] = row
        return carry

    lax.fori_loop(0, 32, list_slots, 0)
    relay(6)
    reduced(5)
    spread(4)
    relay(7)
    reduced(6)
    spread(5)
    forwarded(0)
    reduced(7)
    forwarded(1)

    def rows_complete():
        for _, to_sister in streams:
            for copy in to_sister:
                copy.wait_recv()

    def memory_of(n, cols):
        stored = stored_ref[n]
        live = jnp.logical_and(stored >= 0, stored // 32 == plane).astype(F32)
        row = (stored + 32) % 32
        return rows[row // 4, 0, row % 4, :, cols], rows[row // 4, 1, row % 4, :, cols], live

    def stats_of_spans(first):
        def span(j, carry):
            sequence, place = j // 2, first + j % 2
            i = sequence * 8 + place
            for pair in range(2):
                cols = pl.ds(pair * 256, 256)
                query = two_heads(qg[0, sequence, place, :, cols])
                grad = two_heads(qg[1, sequence, place, :, cols])
                top = jnp.full((1, 128), NEG, F32)
                made = []
                for k in range(2):
                    key, value, live = memory_of(i * 2 + k, cols)
                    score = dot(key, query, 1, 1) * SCALE
                    gw = dot(value, grad, 1, 1)
                    high = jnp.max(score, axis=0, keepdims=True)
                    top = jnp.maximum(top, high * live + NEG * (1.0 - live))
                    made.append((score, gw, live))
                total, inner = 0.0, 0.0
                for k in range(2):
                    score, gw, live = made[k]
                    e = jnp.exp(jnp.minimum(score - top, 0.0)) * live
                    total = total + jnp.sum(e, axis=0, keepdims=True)
                    inner = inner + jnp.sum(e * gw, axis=0, keepdims=True)
                    wide[i * 2 + k, :, pl.ds(pair * 128, 128)] = e.astype(BF)
                    wide[i * 2 + k, :, pl.ds(256 + pair * 128, 128)] = gw.astype(BF)
                line = pl.ds(first * 8 + j * 2 + pair, 1)
                held[ring_z.me, 0, line, :] = top
                held[ring_z.me, 1, line, :] = total
                held[ring_z.me, 2, line, :] = inner
            return carry

        lax.fori_loop(0, 8, span, 0)

    def exchange_of(u):
        def slot(i, half=None):
            return held.at[i, :, pl.ds(u * 16, 16) if half is None else pl.ds(u * 16 + half * 8, 8)]

        return Gather(copies, ring_z, slot)

    exchanges = [exchange_of(u) for u in range(4)]

    def unit_stats(u):
        units[u][1].end()
        units[4 + u][1].end()
        stats_of_spans(2 * u)

    def exchange_start(u):
        exchanges[u].start(exchanges[u].slot(ring_z.me))

    def exchange_relay(u):
        exchanges[u].relay()

    def exchange_end(u):
        exchanges[u].end()
        here = pl.ds(u * 16, 16)
        tops = [held[k, 0, here] for k in range(4)]
        top = jnp.maximum(jnp.maximum(tops[0], tops[1]), jnp.maximum(tops[2], tops[3]))
        fades = [jnp.exp(t - top) for t in tops]
        total = sum(fades[k] * held[k, 1, here] for k in range(4))
        inner = sum(fades[k] * held[k, 2, here] for k in range(4))
        stats[0, here] = jnp.exp(held[ring_z.me, 0, here] - top) / total
        stats[1, here] = inner / total

    def first_sends_done(u):
        units[u][0].sent()
        units[4 + u][0].sent()


    def attend_spans(first):
        def span(j, carry):
            sequence, place = j // 2, first + j % 2
            i = sequence * 8 + place
            for pair in range(2):
                cols = pl.ds(pair * 256, 256)
                line = pl.ds(first * 8 + j * 2 + pair, 1)
                share = stats[0, line, :]
                center = stats[1, line, :]
                keys, values, ws, dss = [], [], [], []
                for k in range(2):
                    key, value, _ = memory_of(i * 2 + k, cols)
                    lane_w, lane_s = pl.ds(pair * 128, 128), pl.ds(256 + pair * 128, 128)
                    w = wide[i * 2 + k, :, lane_w].astype(F32) * share
                    gw = wide[i * 2 + k, :, lane_s].astype(F32)
                    ds = (w * (gw - center) * SCALE).astype(BF)
                    w = w.astype(BF)
                    wide[i * 2 + k, :, lane_w] = w
                    wide[i * 2 + k, :, lane_s] = ds
                    keys.append(key)
                    values.append(value)
                    ws.append(w)
                    dss.append(ds)
                for which, probs, memory in ((0, ws, values), (1, dss, keys)):
                    out = dot(jnp.concatenate(probs, axis=0), jnp.concatenate(memory, axis=0), 0, 0)
                    for h in range(2):
                        part[which, sequence, place, :, pl.ds(pair * 256 + h * HD, HD)] = out[
                            h * SPAN : (h + 1) * SPAN, h * HD : (h + 1) * HD
                        ].astype(BF)
            return carry

        lax.fori_loop(0, 8, span, 0)

    def row_grads(block):
        for pair in range(2):
            cols = pl.ds(pair * 256, 256)
            for kv in range(2):
                made = []
                for sequence in range(4):
                    n = block * 4 + sequence
                    first, second = table_ref[0, n], table_ref[1, n]
                    both = (table_ref[2, n] >= 2).astype(F32)
                    place = pl.ds((256 if kv == 0 else 0) + pair * 128, 128)
                    probs = jnp.concatenate(
                        [
                            wide[sequence * 16 + first, :, place],
                            wide[sequence * 16 + second, :, place] * both.astype(BF),
                        ],
                        axis=1,
                    )
                    other = jnp.concatenate(
                        [
                            two_heads(qg[kv, sequence, first // 2, :, cols]),
                            two_heads(qg[kv, sequence, second // 2, :, cols]),
                        ],
                        axis=0,
                    )
                    made.append(dot(probs, other, 1, 0).astype(BF))
                for r in range(4):
                    total = None
                    for sequence in range(4):
                        n = block * 4 + sequence
                        pick = jnp.logical_and(table_ref[2, n] >= 1, table_ref[3, n] == r)
                        term = made[sequence] * pick.astype(F32).astype(BF)
                        total = term if total is None else total + term
                    rows[block, kv, r, :, cols] = total


    def z_unit(w, u):
        reduce = Reduce(
            copies,
            ring_z,
            lambda i, half: part.at[w, i, 2 * u + half],
            lambda half: tmp.at[w, 2 * u + half],
            lambda k: got.at[w, k // 2, 2 * u + k % 2],
        )

        def slot(i, half=None):
            return v_enc.at[w, i, pl.ds(2 * u, 2)] if half is None else v_enc.at[w, i, 2 * u + half]

        return reduce, Gather(copies, ring_x, slot)

    outs = [[z_unit(w, u) for u in range(4)] for w in range(2)]

    def zb(w, u):
        outs[w][u][0].start()

    def zr(w, u):
        outs[w][u][0].relay(add_rows)

    def zd(w, u):
        reduce, gather = outs[w][u]
        reduce.end(add_rows, lambda half: gather.slot(ring_x.me, half))
        gather.start(gather.slot(ring_x.me))

    def zs(w, u):
        outs[w][u][1].relay()


    order = (ring_y.far, ring_y.p, ring_y.q, ring_y.me)

    def y_unit(t):
        here = pl.ds(t * TC, TC)
        by_row = Reduce(
            copies,
            ring_y,
            lambda i, half: rows.at[i * 2 + c, half, :, here],
            lambda half: y_tmp.at[half, t],
            lambda k: y_got.at[k, t],
        )
        by_group = Reduce(
            copies,
            ring_x,
            lambda i, half: qg.at[half, :, i * 2 + t * TC // SPAN, pl.ds(t * TC % SPAN, TC)],
            lambda half: x_tmp.at[half, t],
            lambda k: x_got.at[k, t],
        )
        return by_row, by_group

    chunks = [y_unit(t) for t in range(CHUNKS)]
    swaps = []

    def sister_rows(k):
        block = order[k] * 2 + 1 - c
        row_grads(block)
        swaps.append(copies.push(rows.at[block], c_got.at[order[k]], sister))

    def own_rows(k):
        row_grads(order[k] * 2 + c)

    def y_start(t):
        here = pl.ds(t * TC, TC)
        for k, i in enumerate(order):
            if t == 0:
                swaps[k].wait_recv()
            for half in range(2):
                block = rows.at[i * 2 + c, half, :, here]
                add_rows(block, block, c_got.at[i, half, :, here])
        chunks[t][0].start()

    def y_relay(t):
        chunks[t][0].relay(add_rows)

    def y_done(t):
        chunks[t][0].end(add_rows, lambda half: mine.at[half])

        def tile(j, carry):
            cols = pl.ds(pl.multiple_of(j * 512, 512), 512)
            keys = mine[0].reshape(4 * TC, 512)
            values = mine[1].reshape(4 * TC, 512)
            product = dot(keys, v_wk[cols, :], 1, 1) + dot(values, v_wv[cols, :], 1, 1)
            product = product.astype(BF)
            for r in range(4):
                qg[j // 4, j % 4, r * 2 + t * TC // SPAN, pl.ds(t * TC % SPAN, TC), :] = product[r * TC : (r + 1) * TC]
            return carry

        lax.fori_loop(0, 8, tile, 0)
        chunks[t][1].start()

    def x_relay(t):
        chunks[t][1].relay(add_rows)

    def result(t):
        unit = chunks[t][1]
        for copy in unit.near:
            copy.wait_recv()
        for half in range(2):
            for j in range(4):
                cols = pl.ds(half * 2048 + j * 512, 512)
                terms = (unit.part(ring_x.me, half)[j], x_got[half, t, j], x_got[2 + half, t, j])
                grad_encoded[pl.ds(t * TC, TC), cols] = add_up(terms)

    rows_complete()
    unit_stats(0)
    exchange_start(0)
    spread(6)
    unit_stats(1)
    exchange_relay(0)
    exchange_start(1)
    spread(7)
    early = list(copies.started.values())
    exchange_end(0)
    first_sends_done(0)
    attend_spans(0)
    zb(0, 0)
    exchange_relay(1)
    unit_stats(2)
    exchange_start(2)
    exchange_end(1)
    first_sends_done(1)
    attend_spans(2)
    zr(0, 0)
    zb(1, 0)
    exchange_relay(2)
    unit_stats(3)
    exchange_start(3)
    exchange_end(2)
    first_sends_done(2)
    zd(0, 0)
    attend_spans(4)
    zr(1, 0)
    zb(0, 1)
    exchange_relay(3)
    exchange_end(3)
    first_sends_done(3)
    zd(1, 0)
    attend_spans(6)
    zr(0, 1)
    zb(1, 1)
    for copy in early:
        copies.settle(copy)
    sister_rows(0)
    zs(0, 0)
    zd(0, 1)
    sister_rows(1)
    zr(1, 1)
    zb(0, 2)
    sister_rows(2)
    zs(1, 0)
    sister_rows(3)
    zd(1, 1)
    zr(0, 2)
    zb(1, 2)
    own_rows(0)
    own_rows(1)
    zs(0, 1)
    zd(0, 2)
    zr(1, 2)
    own_rows(2)
    own_rows(3)
    zb(0, 3)
    again = load_wide(0) + load_wide(1)
    y_start(0)
    zs(1, 1)
    zd(1, 2)
    zr(0, 3)
    zb(1, 3)
    zs(0, 2)
    zd(0, 3)
    y_relay(0)
    y_start(1)
    zs(1, 2)
    zr(1, 3)
    zd(1, 3)
    y_done(0)
    zs(0, 3)
    y_relay(1)
    x_relay(0)
    zs(1, 3)
    y_done(1)
    for load in again:
        load.wait()
    for u in range(4):
        outs[0][u][1].end()

    def everyone(w, g, first, size):
        return v_enc[w, g, pl.ds(first // SPAN, size // SPAN)].reshape(size, 512)

    def attended_tile(j, carry):
        cols = pl.ds(pl.multiple_of(j % 2 * 256, 256), 256)
        total = None
        for g in range(4):
            weight = wide[pl.ds(32 + j // 2 * 16 + g * 4, 4), :, cols].reshape(512, 256)
            term = dot(everyone(0, g, 0, 512), weight, 1, 0)
            total = term if total is None else total + term
        v_hid[:, pl.ds(pl.multiple_of(j * 256, 256), 256)] = total.astype(BF)
        return carry

    def hidden_rows(first):
        def tile(j, carry):
            total = None
            for g in range(4):
                weight = wide[pl.ds(g * 8 + j * 2, 2)].reshape(256, 512)
                term = dot(everyone(1, g, first, 256), weight, 1, 1)
                total = term if total is None else total + term
            v_gout[pl.ds(first, 256), pl.ds(pl.multiple_of(j * 256, 256), 256)] = total.astype(BF)
            return carry

        lax.fori_loop(0, 4, tile, 0)

    def shift_down(out, ref, t):
        first = max(t - 1, 0) * 128
        row = lax.broadcasted_iota(jnp.int32, (128, 256), 0) + (t * 128 - (SPAN - 1) - first)
        col = lax.broadcasted_iota(jnp.int32, (128, 256), 1)
        move = (row == col).astype(BF)
        out[pl.ds(t * 128, 128), :] = dot(move, ref[pl.ds(first, 256), :], 1, 0).astype(BF)

    lax.fori_loop(0, 4, attended_tile, 0)
    for t in range(4):
        shift_down(attended, v_hid, t)
    x_relay(1)
    result(0)
    for u in range(2):
        outs[1][u][1].end()
    hidden_rows(0)
    for t in range(2):
        shift_down(grad_hidden, v_gout, t)
    for u in range(2, 4):
        outs[1][u][1].end()
    hidden_rows(256)
    for t in range(2, 4):
        shift_down(grad_hidden, v_gout, t)
    result(1)
    copies.finish()


def cross_attention(loc, hid, wq, enc, wk, wv, gout, wo, ids):
    return pl.pallas_call(
        kernel,
        out_shape=[
            jax.ShapeDtypeStruct((512, 1024), BF),
            jax.ShapeDtypeStruct((512, 1024), BF),
            jax.ShapeDtypeStruct((NTOK, 4096), BF),
            jax.ShapeDtypeStruct((4, 8, 128), jnp.int32),
        ],
        in_specs=[SM] + [ANY] * 8,
        out_specs=[VM, VM, VM, ANY],
        scratch_shapes=[
            pltpu.VMEM((512, 1024), BF),
            pltpu.VMEM((512, 1024), BF),
            pltpu.VMEM((512, 1024), BF),
            pltpu.VMEM((64, 128, 512), BF),
            pltpu.VMEM((4096, 512), BF),
            pltpu.VMEM((4096, 512), BF),
            pltpu.VMEM((2, 4, SPANS, SPAN, 512), BF),
            pltpu.VMEM((2, 4, SPANS, SPAN, 512), BF),
            pltpu.VMEM((2, SPANS, SPAN, 512), BF),
            pltpu.VMEM((2, 2, SPANS, SPAN, 512), BF),
            pltpu.VMEM((2, 4, SPANS, SPAN, 512), BF),
            pltpu.VMEM((8, 2, 4, NTOK, 512), BF),
            pltpu.SMEM((4, 8, 128), jnp.int32),
            pltpu.SMEM((64,), jnp.int32),
            pltpu.SMEM((4, 32), jnp.int32),
            pltpu.VMEM((2, 64, 128), F32),
            pltpu.VMEM((4, 3, 64, 128), F32),
            pltpu.VMEM((4, 2, 4, NTOK, 512), BF),
            pltpu.VMEM((2, CHUNKS, 4, TC, 512), BF),
            pltpu.VMEM((4, CHUNKS, 4, TC, 512), BF),
            pltpu.VMEM((2, 4, TC, 512), BF),
            pltpu.VMEM((2, CHUNKS, 4, TC, 512), BF),
            pltpu.VMEM((4, CHUNKS, 4, TC, 512), BF),
            pltpu.SemaphoreType.DMA((272,)),
            pltpu.SemaphoreType.DMA((272,)),
            pltpu.SemaphoreType.DMA((40,)),
        ],
        compiler_params=pltpu.CompilerParams(
            collective_id=0, has_side_effects=True, vmem_limit_bytes=62 << 20
        ),
        name="cross_attention",
    )(loc, hid, wq, enc, wk, wv, gout, wo, ids)


def two_heads(block):
    zero = jnp.zeros((SPAN, HD), BF)
    return jnp.concatenate(
        [
            jnp.concatenate([block[:, :HD], zero], axis=1),
            jnp.concatenate([zero, block[:, HD:]], axis=1),
        ],
        axis=0,
    )


def body(
    hidden, query_weight, key_weight, value_weight, output_weight,
    encoded, location, neighbours, pattern, grad_out,
):
    ids = jnp.pad(neighbours + 256 * pattern, ((0, 0), (0, 126)))
    attended, grad_hidden, grad_encoded, _ = cross_attention(
        location, hidden, query_weight.reshape(8, 128, 2048), encoded.reshape(8, 64, 4096),
        key_weight, value_weight, grad_out, output_weight.reshape(16, 128, 1024), ids,
    )
    return attended, grad_hidden, grad_encoded.reshape(1, NTOK, 4096)


def solution(mesh):
    return jax.shard_map(
        body,
        mesh=mesh,
        in_specs=(
            P("dp", "head"),
            P("head", None),
            P(None, "head"),
            P(None, "head"),
            P(None, "head"),
            P("dp", None, None),
            P(),
            P("dp", None),
            P("dp", None),
            P("dp", "head"),
        ),
        out_specs=(P("dp", "head"), P("dp", "head"), P(("dp", "head"), None, None)),
        check_vma=False,
    )
```
